32 devices in a mesh: groups: 2 (over y), seq: 16 (over z, x, core).
Axes of the slice: x: 2, y: 2, z: 4, core: 2. Of those that a mesh axis runs over, the one named last changes fastest.
Arguments:
- hidden: bfloat16 [4, 4, 8192], P('groups', None, 'seq'), parts along dimension 0, may hold values from -1200 to 1200
- norm_gain: bfloat16 [8192], P('seq'), may hold values from 0.099609375 to 1.8984375
- q_weight: bfloat16 [8192, 8192], P('seq'), may hold values from -0.0625 to 0.0625
- kv_weight: bfloat16 [8192, 2048], P('seq'), may hold values from -0.0625 to 0.0625
- out_weight: bfloat16 [8192, 8192], P('seq'), may hold values from -0.09375 to 0.09375
- head_kind: int32 [8], replicated, may hold values from 0 to 1, as said below
- ret_keys: bfloat16 [4, 4, 32768, 128], P('groups', None, 'seq'), parts along dimension 0, may hold values from -600 to 600
- ret_values: bfloat16 [4, 4, 32768, 128], P('groups', None, 'seq'), parts along dimension 0, may hold values from -8 to 8
- stream_keys: bfloat16 [4, 4, 2048, 128], P('groups', None, 'seq'), parts along dimension 0, may hold values from -600 to 600
- stream_values: bfloat16 [4, 4, 2048, 128], P('groups', None, 'seq'), parts along dimension 0, may hold values from -8 to 8
- cache_len: int32 [4], P('groups'), parts along dimension 0, may hold values from 1 to 32768, as said below
- sink_len: int32 [4], P('groups'), parts along dimension 0, may hold values from 1 to 128, as said below
- window_len: int32 [4], P('groups'), parts along dimension 0, may hold values from 1 to 1920, as said below
Outputs:
- layer_output: bfloat16 [4, 4, 8192], P('groups', None, 'seq'), parts along dimension 0
- new_entries: bfloat16 [4, 4, 2048], P('groups'), parts along dimension 0
The draws below stay inside these ranges and needn't reach their ends.
There are 2 independent parts, one for each index of `groups`. The reference program is written for one: setup_inputs(seed, part) draws one part's arguments, and reference() takes and returns one part's arrays. A program takes and returns all parts, laid end to end along the dimension named above; an argument that names none is the same for every part. Nothing has to cross between parts.
Inputs may be any that keep to these rules, and one draw needn't show every extreme that they name: `head_kind`: exactly 4 of the 8 entries are 1, the others 0. `cache_len`: in every draw some request has all 32768 positions filled. `sink_len`: in every draw some request holds 128 sink tokens. `window_len`: in every draw some request holds 1920 recent tokens.
All inputs are finite; a program needn't handle non-finite values.
Results may differ from the reference program's by a relative error of at most 0.0075.
The reference program's roundings to bfloat16 on the way (of `normed`, `queries`, `rounded` and `attention`) count: a program that leaves them out, or rounds other values in their place, can miss the bound.
Values may be sent and summed in bfloat16 or wider, within the bound.
A program may use at most 128 MiB of HBM per device.

```python
import math
import jax
import jax.numpy as jnp
from jax import lax

D = 8192
H = 64
KVH = 8
HD = 128
RET = 4
STR = 4
REQS = 2
DRAFT = 4
CACHE_DEV = 2048
CACHE_LEN = 32768
SLOTS = 2048
SINK_CAP = 128
N_SEQ = 16


def draw_hidden(key, part):
    key_list = jax.random.split(key, 3)
    column = jnp.arange(D, dtype=jnp.float32) / (D - 1)
    noise_draw = jnp.clip(jax.random.normal(key_list[0], (REQS, DRAFT, D), jnp.float32), -4.0, 4.0)
    rising = jnp.sqrt(1.0 + 2.0 * column)
    column_scale = jnp.exp(jax.random.uniform(key_list[1], (D,), jnp.float32, 0.0, math.log(10.0)))
    row_scale = jnp.exp(jax.random.uniform(key_list[2], (REQS, DRAFT, 1), jnp.float32, 0.0, math.log(10.0)))
    return (noise_draw * column_scale * rising * row_scale).astype(jnp.bfloat16)


def scaled_keys(key, shape, head_top):
    key_list = jax.random.split(key, 3)
    base_draw = jnp.clip(jax.random.normal(key_list[0], shape, jnp.float32), -5.0, 5.0)
    head_scale = jnp.exp(jax.random.uniform(key_list[1], (shape[0], shape[1], 1, 1), jnp.float32, 0.0, math.log(head_top)))
    slot_scale = jnp.exp(jax.random.uniform(key_list[2], (shape[0], shape[1], shape[2], 1), jnp.float32, math.log(0.3), math.log(3.0)))
    return base_draw * head_scale * slot_scale


def draw_ret_keys(key, part):
    return scaled_keys(key, (REQS, RET, CACHE_LEN, HD), 2.0).astype(jnp.bfloat16)


def draw_stream_keys(key, part):
    return scaled_keys(key, (REQS, STR, SLOTS, HD), 2.0).astype(jnp.bfloat16)


def draw_head_kind(key, part):
    shuffled = jax.random.permutation(key, KVH)
    return (shuffled < RET).astype(jnp.int32)


def filled_counts(key, most):
    chosen = jax.random.randint(jax.random.fold_in(key, 7), (), 0, REQS)
    others = jax.random.randint(jax.random.fold_in(key, 11), (REQS,), 1, most + 1)
    return jnp.where(jnp.arange(REQS) == chosen, most, others).astype(jnp.int32)


def draw_cache_len(key, part):
    return filled_counts(key, CACHE_LEN)


def draw_sink_len(key, part):
    return filled_counts(key, SINK_CAP)


def draw_window_len(key, part):
    return filled_counts(key, SLOTS - SINK_CAP)


def spiked(drawn, rng, source, target, blocks, factor):
    owner, partner = [(jnp.arange(drawn.shape[axis_at]) // (drawn.shape[axis_at] // blocks)).reshape([-1 if axis == axis_at else 1 for axis in range(drawn.ndim)]) for axis_at in (source, target)]
    chosen = jax.random.permutation(rng, blocks)[partner]
    strong = (owner == chosen) | (owner == (partner + blocks // 2) % blocks)
    return jnp.where(strong, factor * drawn, drawn)


def shard_levels(key, dims, cuts, smallest, largest):
    def one(axis_at, parts):
        heights = jax.random.uniform(jax.random.fold_in(jax.random.fold_in(key, 6), axis_at), (parts,), jnp.float32, smallest / len(cuts), largest / len(cuts))
        return jnp.repeat(jnp.exp(heights), dims[axis_at] // parts).reshape((-1,) + (1,) * (len(dims) - axis_at - 1))

    gain = one(*cuts[0])
    for cut in cuts[1:]:
        gain = gain * one(*cut)
    return gain


def normal_values(own_key, shape, width, most, cuts=(), kind=jnp.bfloat16):
    drawn = jax.random.normal(own_key, shape, jnp.float32) * width
    if len(cuts) > 0:
        drawn = shard_levels(own_key, shape, cuts, -0.22, 0.18) * drawn
    return jnp.clip(drawn, min=-most, max=most).astype(kind)


def gaussian_with(rng, dims, spread, limit, shards, heavy, kind=jnp.bfloat16):
    array = spread * jax.random.normal(rng, dims, jnp.float32)
    if shards:
        array = array * shard_levels(rng, dims, shards, -0.22, 0.18)
    return jnp.clip(spiked(array, jax.random.fold_in(rng, 3), *heavy), -limit, limit).astype(kind)


def setup_inputs(seed: int = 0, part: int = 0) -> dict:
    arg_keys = jax.random.split(jax.random.key(seed), 14)
    own_keys = jax.random.split(jax.random.fold_in(arg_keys[13], part), 14)
    return {
        "hidden": draw_hidden(jax.random.fold_in(jax.random.fold_in(arg_keys[13], part), 71), part),
        "norm_gain": jnp.clip(1.0 + 0.18 * jax.random.normal(arg_keys[1], (D,), jnp.float32), 0.099609375, 1.8984375).astype(jnp.bfloat16),
        "q_weight": normal_values(arg_keys[2], (D, H * HD), D ** -0.5, 0.0625, ((0, 16),)),
        "kv_weight": normal_values(arg_keys[3], (D, 2 * KVH * HD), D ** -0.5, 0.0625, ((0, 16),)),
        "out_weight": gaussian_with(arg_keys[4], (H * HD, D), (H * HD) ** -0.5, 0.09375, ((0, 16),), (0, 1, 16, 2.0)),
        "head_kind": draw_head_kind(jax.random.fold_in(arg_keys[13], 71), part),
        "ret_keys": draw_ret_keys(jax.random.fold_in(jax.random.fold_in(arg_keys[13], part), 71), part),
        "ret_values": normal_values(own_keys[7], (REQS, RET, CACHE_LEN, HD), 2.0, 8.0, ((2, 16),)),
        "stream_keys": draw_stream_keys(jax.random.fold_in(jax.random.fold_in(arg_keys[13], part), 71), part),
        "stream_values": normal_values(own_keys[9], (REQS, STR, SLOTS, HD), 2.0, 8.0, ((2, 16),)),
        "cache_len": draw_cache_len(jax.random.fold_in(jax.random.fold_in(arg_keys[13], part), 71), part),
        "sink_len": draw_sink_len(jax.random.fold_in(jax.random.fold_in(arg_keys[13], part), 71), part),
        "window_len": draw_window_len(jax.random.fold_in(jax.random.fold_in(arg_keys[13], part), 71), part),
    }


epsilon = 1e-05
floor_score = -1e+30

def block_stats(queries, cache_keys, cache_values, visible, score_scale):
    scores = jnp.einsum('bhqd,bhld->bhql', queries.astype(jnp.float32), cache_keys.astype(jnp.float32)) * score_scale
    scores = jnp.where(visible, scores, floor_score)
    peak_score = lax.optimization_barrier(jnp.max(scores, axis=-1))
    weights = jnp.where(visible, jnp.exp(scores - peak_score[..., None]), 0.0)
    weight_total = lax.optimization_barrier(jnp.sum(weights, axis=-1))
    rounded = lax.optimization_barrier(weights.astype(jnp.bfloat16))
    block_out = jnp.einsum('bhql,bhld->bhqd', rounded.astype(jnp.float32), cache_values.astype(jnp.float32))
    return (peak_score, weight_total, block_out)

def reference(hidden, norm_gain, q_weight, kv_weight, out_weight, head_kind, ret_keys, ret_values, stream_keys, stream_values, cache_len, sink_len, window_len):
    hidden32 = hidden.astype(jnp.float32)
    inverse = lax.rsqrt(lax.optimization_barrier(jnp.mean(hidden32 * hidden32, axis=-1, keepdims=True)) + epsilon)
    normed = (hidden32 * inverse * norm_gain.astype(jnp.float32)).astype(jnp.bfloat16)
    flat_rows = normed.reshape(REQS * DRAFT, D)
    queries = jnp.dot(flat_rows, q_weight, preferred_element_type=jnp.float32).astype(jnp.bfloat16)
    new_entries = jnp.dot(flat_rows, kv_weight, preferred_element_type=jnp.float32).astype(jnp.bfloat16)
    group_size = H // KVH
    query_rows = DRAFT * group_size
    grouped = queries.reshape(REQS, DRAFT, KVH, group_size, HD).transpose(0, 2, 1, 3, 4).reshape(REQS, KVH, query_rows, HD)
    fresh_split = new_entries.reshape(REQS, DRAFT, 2, KVH, HD)
    new_keys = fresh_split[:, :, 0].transpose(0, 2, 1, 3)
    new_values = fresh_split[:, :, 1].transpose(0, 2, 1, 3)
    order_key = (1 - head_kind) * KVH + jnp.arange(KVH, dtype=jnp.int32)
    head_order = jnp.argsort(order_key).astype(jnp.int32)
    ret_heads = head_order[:RET]
    str_heads = head_order[RET:]
    score_scale = HD ** (-0.5)
    ret_queries = grouped[:, ret_heads]
    str_queries = grouped[:, str_heads]
    slot_block = SLOTS // N_SEQ

    def retrieval_block(block_index):
        first_pos = block_index * CACHE_DEV
        keys_block = lax.dynamic_slice_in_dim(ret_keys, first_pos, CACHE_DEV, 2)
        values_block = lax.dynamic_slice_in_dim(ret_values, first_pos, CACHE_DEV, 2)
        positions = first_pos + jnp.arange(CACHE_DEV, dtype=jnp.int32)
        visible = (positions[None, :] < cache_len[:, None])[:, None, None, :]
        return block_stats(ret_queries, keys_block, values_block, visible, score_scale)

    def running_block(block_index):
        first_pos = block_index * slot_block
        keys_block = lax.dynamic_slice_in_dim(stream_keys, first_pos, slot_block, 2)
        values_block = lax.dynamic_slice_in_dim(stream_values, first_pos, slot_block, 2)
        positions = (first_pos + jnp.arange(slot_block, dtype=jnp.int32))[None, :]
        sinks = positions < sink_len[:, None]
        recent = (positions >= SINK_CAP) & (positions < SINK_CAP + window_len[:, None])
        visible = (sinks | recent)[:, None, None, :]
        return block_stats(str_queries, keys_block, values_block, visible, score_scale)
    block_ids = jnp.arange(N_SEQ, dtype=jnp.int32)
    ret_peak, ret_total, ret_out = lax.map(retrieval_block, block_ids)
    str_peak, str_total, str_out = lax.map(running_block, block_ids)
    peak_all = jnp.zeros((N_SEQ, REQS, KVH, query_rows), jnp.float32).at[:, :, ret_heads].set(ret_peak).at[:, :, str_heads].set(str_peak)
    total_all = jnp.zeros((N_SEQ, REQS, KVH, query_rows), jnp.float32).at[:, :, ret_heads].set(ret_total).at[:, :, str_heads].set(str_total)
    out_all = jnp.zeros((N_SEQ, REQS, KVH, query_rows, HD), jnp.float32).at[:, :, ret_heads].set(ret_out).at[:, :, str_heads].set(str_out)
    token_of_row = jnp.arange(query_rows, dtype=jnp.int32) // group_size
    new_visible = jnp.arange(DRAFT, dtype=jnp.int32)[None, :] <= token_of_row[:, None]
    new_peak, new_total, new_out = block_stats(grouped, new_keys, new_values, new_visible, score_scale)
    top_score = jnp.maximum(lax.optimization_barrier(jnp.max(peak_all, axis=0)), new_peak)
    cache_factor = jnp.exp(peak_all - top_score[None])
    new_factor = jnp.exp(new_peak - top_score)
    denominator = lax.optimization_barrier(jnp.sum(cache_factor * total_all, axis=0)) + new_factor * new_total
    numerator = lax.optimization_barrier(jnp.sum(cache_factor[..., None] * out_all, axis=0)) + new_factor[..., None] * new_out
    attended = numerator / denominator[..., None]
    attention = attended.reshape(REQS, KVH, DRAFT, group_size, HD).transpose(0, 2, 1, 3, 4).reshape(REQS * DRAFT, H * HD).astype(jnp.bfloat16)
    layer_output = jnp.dot(attention, out_weight, preferred_element_type=jnp.float32).astype(jnp.bfloat16)
    return (layer_output.reshape(REQS, DRAFT, D), new_entries.reshape(REQS, DRAFT, 2 * KVH * HD))
```

```python
import math

import jax
import jax.numpy as jnp
from jax import lax
from jax.experimental import pallas as pl
from jax.experimental.pallas import tpu as pltpu
from jax.sharding import PartitionSpec as P

SINK_CAP = 128
MESH = pl.DeviceIdType.MESH


epsilon = 1e-05
floor_score = -1e30


def joined(part, axis, combine):
    gathered = jax.tree.map(lambda a: lax.all_gather(a, axis), part)

    def take(source):
        return jax.tree.map(lambda a: lax.dynamic_index_in_dim(a, source, 0, False), gathered)

    return lax.fori_loop(
        1, lax.axis_size(axis), lambda source, state: combine(state, take(source)), take(0)
    )


def block_stats(queries, cache_keys, cache_values, visible, score_scale):
    scores = (
        jnp.einsum("bhqd,bhld->bhql", queries, cache_keys, preferred_element_type=jnp.float32)
        * score_scale
    )
    scores = jnp.where(visible, scores, floor_score)
    peak_score = jnp.max(scores, axis=-1)
    weights = jnp.where(visible, jnp.exp(scores - peak_score[..., None]), 0.0)
    weight_total = jnp.sum(weights, axis=-1)
    block_out = jnp.einsum(
        "bhql,bhld->bhqd",
        weights.astype(jnp.bfloat16),
        cache_values,
        preferred_element_type=jnp.float32,
    )
    return (peak_score, weight_total, block_out)


def spread_rows(values_in, selector):
    return jnp.einsum("brq,gr->bgq", values_in, selector, precision=lax.Precision.HIGHEST)


def spread_vectors(values_in, selector):
    return jnp.einsum("brqd,gr->bgqd", values_in, selector, precision=lax.Precision.HIGHEST)


def join_parts(first_part, second_part):
    top_score = jnp.maximum(first_part[0], second_part[0])
    left_factor = jnp.exp(first_part[0] - top_score)
    right_factor = jnp.exp(second_part[0] - top_score)
    joined_total = first_part[1] * left_factor + second_part[1] * right_factor
    joined_out = first_part[2] * left_factor[..., None] + second_part[2] * right_factor[..., None]
    return (top_score, joined_total, joined_out)


def per_device(
    hidden,
    norm_gain,
    q_weight,
    kv_weight,
    out_weight,
    head_kind,
    ret_keys,
    ret_values,
    stream_keys,
    stream_values,
    cache_len,
    sink_len,
    window_len,
):
    requests, drafts, local_width = hidden.shape
    kv_heads = head_kind.shape[0]
    head_dim = ret_keys.shape[3]
    retrieval = ret_keys.shape[1]
    running = stream_keys.shape[1]
    head_count = q_weight.shape[1] // head_dim
    group_size = head_count // kv_heads
    query_rows = drafts * group_size
    devices = lax.axis_size("seq")
    position = lax.axis_index("seq")
    tokens = requests * drafts
    hidden32 = hidden.astype(jnp.float32)
    squares = lax.psum(jnp.sum(hidden32 * hidden32, axis=-1), "seq")
    inverse = lax.rsqrt(squares / (local_width * devices) + epsilon)
    normed = (hidden32 * inverse[..., None] * norm_gain.astype(jnp.float32)).astype(jnp.bfloat16)
    flat_rows = normed.reshape(tokens, local_width)
    part_query = jnp.dot(flat_rows, q_weight, preferred_element_type=jnp.float32)
    part_fresh = jnp.dot(flat_rows, kv_weight, preferred_element_type=jnp.float32)
    whole_query, whole_fresh = lax.psum((part_query, part_fresh), "seq")
    queries = whole_query.astype(jnp.bfloat16)
    new_entries = whole_fresh.astype(jnp.bfloat16)
    grouped = (
        queries.reshape(requests, drafts, kv_heads, group_size, head_dim)
        .transpose(0, 2, 1, 3, 4)
        .reshape(requests, kv_heads, query_rows, head_dim)
    )
    fresh_split = new_entries.reshape(requests, drafts, 2, kv_heads, head_dim)
    new_keys = fresh_split[:, :, 0].transpose(0, 2, 1, 3)
    new_values = fresh_split[:, :, 1].transpose(0, 2, 1, 3)
    kind_flag = head_kind == 1
    rank_ret = jnp.cumsum(head_kind) - 1
    rank_str = jnp.cumsum(1 - head_kind) - 1
    select_ret = (
        kind_flag[:, None] & (rank_ret[:, None] == jnp.arange(retrieval)[None, :])
    ).astype(jnp.float32)
    select_str = (
        jnp.logical_not(kind_flag)[:, None] & (rank_str[:, None] == jnp.arange(running)[None, :])
    ).astype(jnp.float32)
    ret_queries = jnp.einsum(
        "bgqd,gr->brqd",
        grouped,
        select_ret.astype(jnp.bfloat16),
        preferred_element_type=jnp.float32,
    ).astype(jnp.bfloat16)
    str_queries = jnp.einsum(
        "bgqd,gr->brqd",
        grouped,
        select_str.astype(jnp.bfloat16),
        preferred_element_type=jnp.float32,
    ).astype(jnp.bfloat16)
    score_scale = head_dim ** (-0.5)
    cache_block = ret_keys.shape[2]
    cache_pos = position * cache_block + jnp.arange(cache_block)
    ret_visible = (cache_pos[None, :] < cache_len[:, None])[:, None, None, :]
    slot_block = stream_keys.shape[2]
    slot_pos = (position * slot_block + jnp.arange(slot_block))[None, :]
    sink_part = slot_pos < sink_len[:, None]
    recent_part = (slot_pos >= SINK_CAP) & (slot_pos < SINK_CAP + window_len[:, None])
    str_visible = (sink_part | recent_part)[:, None, None, :]
    ret_peak, ret_total, ret_out = block_stats(
        ret_queries, ret_keys, ret_values, ret_visible, score_scale
    )
    str_peak, str_total, str_out = block_stats(
        str_queries, stream_keys, stream_values, str_visible, score_scale
    )
    peak_all = spread_rows(ret_peak, select_ret) + spread_rows(str_peak, select_str)
    total_all = spread_rows(ret_total, select_ret) + spread_rows(str_total, select_str)
    out_all = spread_vectors(ret_out, select_ret) + spread_vectors(str_out, select_str)
    token_of_row = jnp.arange(query_rows) // group_size
    new_visible = jnp.arange(drafts)[None, :] <= token_of_row[:, None]
    new_peak, new_total, new_out = block_stats(
        grouped, new_keys, new_values, new_visible, score_scale
    )
    own_width = out_weight.shape[0]
    cache_peak, cache_total, cache_out = joined((peak_all, total_all, out_all), "seq", join_parts)
    top_score = jnp.maximum(cache_peak, new_peak)
    cache_factor = jnp.exp(cache_peak - top_score)
    new_factor = jnp.exp(new_peak - top_score)
    denominator = cache_total * cache_factor + new_total * new_factor
    attended = (
        cache_out * cache_factor[..., None] + new_out * new_factor[..., None]
    ) / denominator[..., None]
    attention = (
        attended.reshape(requests, kv_heads, drafts, group_size, head_dim)
        .transpose(0, 2, 1, 3, 4)
        .reshape(tokens, head_count * head_dim)
        .astype(jnp.bfloat16)
    )
    own_attention = lax.dynamic_slice_in_dim(attention, position * own_width, own_width, 1)
    own_output = lax.psum_scatter(
        lax.dot_general(
            out_weight, own_attention, (((0,), (1,)), ((), ())), preferred_element_type=jnp.float32
        ),
        "seq",
        scatter_dimension=0,
        tiled=True,
    )
    layer_output = own_output.T.reshape(requests, drafts, local_width).astype(jnp.bfloat16)
    return (layer_output, new_entries.reshape(requests, drafts, 2 * kv_heads * head_dim))


def step_kernel(
    kind_ref, clen_ref, slen_ref, wlen_ref, hidden_ref, gain_ref,
    qw_hbm, kvw_hbm, ow_hbm, rk_hbm, rv_hbm, sk_hbm, sv_hbm,
    out_ref, new_ref,
    w_buf, o_buf, rk, rv, sk, sv,
    sq_send, sq_recv, sib_send, sib_recv, rs_send, rs_recv, ag,
    a_res, stat_cols, a_send, a_recv, st_send, st_recv, o_send, o_recv,
    load_sem, cache_sem, send_sem, recv_sem,
):
    f32, bf16 = jnp.float32, jnp.bfloat16
    n = lax.axis_size("seq")
    me = lax.axis_index("seq")
    core, chip, chips = lax.rem(me, 2), me // 2, n // 2
    sibling = me + 1 - 2 * core
    requests, drafts, width = hidden_ref.shape
    tokens = requests * drafts
    kv_heads = kind_ref.shape[0]
    retrieval, running = rk.shape[1], sk.shape[1]
    head_dim = rk.shape[3]
    own_width = o_buf.shape[1]
    heads = own_width // head_dim
    share = n // kv_heads
    half_rows = heads * drafts
    own_rows = requests * half_rows
    group_rows = share * half_rows
    score_scale = head_dim ** (-0.5)
    exp_scale = score_scale * math.log2(math.e)
    SQ, SIB, RS, AG, ATT, STAT, OUT = range(7)

    def remote(kind, src, dst, send_slot, recv_slot, target):
        return pltpu.make_async_remote_copy(
            src_ref=src, dst_ref=dst,
            send_sem=send_sem.at[kind, send_slot], recv_sem=recv_sem.at[kind, recv_slot],
            device_id={"seq": target}, device_id_type=MESH,
        )

    def peer(step):
        return lax.rem(me + step, n)

    def each_peer(body):
        def run(step, carry):
            body(step, peer(step))
            return carry
        lax.fori_loop(1, n, run, 0)

    def chunk_owner(i):
        other = i < chips
        j = lax.rem(i, chips)
        target_chip = lax.rem(chip + 1 + j, chips)
        return 2 * target_chip + jnp.where(other, 1 - core, core)

    def weight_copies(i):
        p = chunk_owner(i)
        qcols = pl.ds(pl.multiple_of(p * own_width, own_width), own_width)
        kcols = pl.ds(pl.multiple_of(p * head_dim, head_dim), head_dim)
        return (
            pltpu.make_async_copy(qw_hbm.at[:, qcols], w_buf.at[i, :, pl.ds(0, own_width)], load_sem.at[0, i]),
            pltpu.make_async_copy(kvw_hbm.at[:, kcols], w_buf.at[i, :, pl.ds(own_width, head_dim)], load_sem.at[1, i]),
        )

    def out_copy(i):
        p = lax.rem(me + 1 + i, n)
        cols = pl.ds(pl.multiple_of(p * width, width), width)
        return pltpu.make_async_copy(ow_hbm.at[:, cols], o_buf.at[i], load_sem.at[2, i])

    def start_weights(i, carry):
        for copy in weight_copies(i):
            copy.start()
        return carry

    lax.fori_loop(0, n, start_weights, 0)

    barrier = pltpu.get_barrier_semaphore()
    each_peer(lambda step, target: pl.semaphore_signal(
        barrier, inc=1, device_id={"seq": target}, device_id_type=MESH))

    hidden32 = jnp.concatenate([hidden_ref[b].astype(f32) for b in range(requests)], axis=0)
    squares = jnp.sum(hidden32 * hidden32, axis=-1, keepdims=True)
    eye = (lax.broadcasted_iota(jnp.int32, (tokens, 128), 0)
           == lax.broadcasted_iota(jnp.int32, (tokens, 128), 1))
    sq_send[...] = jnp.sum(jnp.where(eye, squares, 0.0), axis=0, keepdims=True)
    sq_recv[me] = sq_send[...]
    stat_cols[...] = jnp.zeros_like(stat_cols)
    pl.semaphore_wait(barrier, n - 1)

    def sq_copy(step, target, source):
        return remote(SQ, sq_send, sq_recv.at[source], step, source, target)

    each_peer(lambda step, target: sq_copy(step, target, me).start())

    cache_copies = [
        (pltpu.make_async_copy(sk_hbm, sk, cache_sem.at[0, 0]),
         pltpu.make_async_copy(sv_hbm, sv, cache_sem.at[1, 0])),
    ]
    for b in range(requests):
        cache_copies.append(
            (pltpu.make_async_copy(rk_hbm.at[b], rk.at[b], cache_sem.at[0, 1 + b]),
             pltpu.make_async_copy(rv_hbm.at[b], rv.at[b], cache_sem.at[1, 1 + b])))
    for pair in cache_copies:
        for copy in pair:
            copy.start()

    each_peer(lambda step, source: sq_copy(step, source, source).wait_recv())
    total_row = sq_recv[0]
    for s in range(1, n):
        total_row = total_row + sq_recv[s]
    total_sq = jnp.sum(jnp.where(eye, total_row, 0.0), axis=1, keepdims=True)
    inverse = lax.rsqrt(total_sq / (width * n) + epsilon)
    normed = (hidden32 * inverse * gain_ref[...].astype(f32)).astype(bf16)

    def project(i):
        for copy in weight_copies(i):
            copy.wait()
        return jnp.dot(normed, w_buf[i], preferred_element_type=f32)

    def sib_copy(j):
        return remote(SIB, sib_send.at[j], sib_recv.at[j], j, j, sibling)

    def first_half(j, carry):
        sib_send[j] = project(j)
        sib_copy(j).start()
        return carry

    lax.fori_loop(0, chips, first_half, 0)

    def rs_copy(j):
        target = 2 * lax.rem(chip + 1 + j, chips) + core
        return remote(RS, rs_send.at[j], rs_recv.at[j], j, j, target)

    def second_half(j, carry):
        value = project(chips + j)
        sib_copy(j).wait_recv()
        rs_send[j] = value + sib_recv[j]
        rs_copy(j).start()
        return carry

    lax.fori_loop(0, chips - 1, second_half, 0)
    own = project(n - 1)
    sib_copy(chips - 1).wait_recv()
    own = own + sib_recv[chips - 1]

    def start_out(i, carry):
        out_copy(i).start()
        return carry

    lax.fori_loop(0, n, start_out, 0)

    for j in range(chips - 1):
        rs_copy(j).wait_recv()
        own = own + rs_recv[j]

    def by_head(values):
        return jnp.concatenate(
            [values[b * drafts:(b + 1) * drafts, h * head_dim:(h + 1) * head_dim]
             for b in range(requests) for h in range(heads)], axis=0)

    packed = jnp.concatenate(
        [by_head(own[:, :own_width]), own[:, own_width:],
         jnp.zeros((ag.shape[1] - own_rows - tokens, head_dim), f32)], axis=0)
    ag[me] = packed.astype(bf16)

    def ag_copy(step, target, source):
        return remote(AG, ag.at[source], ag.at[source], step, source, target)

    each_peer(lambda step, target: ag_copy(step, target, me).start())

    kinds = [kind_ref[g] for g in range(kv_heads)]
    slot_of, before = [], 0
    for g in range(kv_heads):
        slot = jnp.where(kinds[g] == 1, before, retrieval + g - before)
        slot_of.append(jnp.minimum(slot, retrieval + running - 1))
        before = before + kinds[g]
    head_of = []
    for j in range(retrieval + running):
        found = 0
        for g in range(kv_heads):
            found = found + jnp.where(slot_of[g] == j, g, 0)
        head_of.append(jnp.minimum(found, kv_heads - 1))

    each_peer(lambda step, source: ag_copy(step, source, source).wait_recv())

    for p in range(n):
        piece = ag[p, own_rows:, :]
        for b in range(requests):
            new_ref[b, :, p * head_dim:(p + 1) * head_dim] = piece[b * drafts:(b + 1) * drafts]

    def attend(b, j, keys, values, visible):
        q = ag[pl.ds(share * head_of[j], share), b * half_rows:(b + 1) * half_rows, :]
        q = q.reshape(group_rows, head_dim)
        scores = lax.dot_general(q, keys, (((1,), (1,)), ((), ())), preferred_element_type=f32)
        scores = jnp.where(visible, scores, floor_score)
        peak = jnp.max(scores, axis=-1, keepdims=True)
        weights = jnp.exp2((scores - peak) * exp_scale)
        total = jnp.sum(weights, axis=-1, keepdims=True)
        block = jnp.dot(weights.astype(bf16), values, preferred_element_type=f32)
        a_res[j, :, b * half_rows:(b + 1) * half_rows, :] = block.astype(bf16).reshape(
            share, half_rows, head_dim)
        lane = lax.broadcasted_iota(jnp.int32, (half_rows, 128), 1)
        for at, column in ((0, peak * score_scale), (own_rows, total)):
            rows = pl.ds(at + b * half_rows, half_rows)
            kept = stat_cols[rows, :]
            for s in range(share):
                kept = jnp.where(lane == share * head_of[j] + s,
                                 column[s * half_rows:(s + 1) * half_rows], kept)
            stat_cols[rows, :] = kept

    for copy in cache_copies[0]:
        copy.wait()
    slots = sk.shape[2]
    slot_pos = me * slots + lax.broadcasted_iota(jnp.int32, (1, slots), 1)
    positions = rk.shape[2]
    cache_pos = me * positions + lax.broadcasted_iota(jnp.int32, (1, positions), 1)
    for b in range(requests):
        seen = (slot_pos < slen_ref[b]) | (
            (slot_pos >= SINK_CAP) & (slot_pos < SINK_CAP + wlen_ref[b]))
        for r in range(running):
            attend(b, retrieval + r, sk[b, r], sv[b, r], seen)
    for b in range(requests):
        for copy in cache_copies[1 + b]:
            copy.wait()
        seen = cache_pos < clen_ref[b]
        for r in range(retrieval):
            attend(b, r, rk[b, r], rv[b, r], seen)

    stat_rows = stat_cols[...].T
    for p in range(n):
        st_send[p] = stat_rows[p:p + 1, :]
    for g in range(kv_heads):
        a_send[g * share:(g + 1) * share] = a_res[slot_of[g]]
    st_recv[me] = st_send[me]
    a_recv[me] = a_send[me]

    def att_copy(step, target, source):
        return remote(ATT, a_send.at[target], a_recv.at[source], step, source, target)

    def st_copy(step, target, source):
        return remote(STAT, st_send.at[target], st_recv.at[source], step, source, target)

    def send_attention(step, target):
        st_copy(step, target, me).start()
        att_copy(step, target, me).start()

    each_peer(send_attention)

    own_head = me // share
    own_q = ag[me, 0:own_rows, :]
    new_keys = ag[own_head, own_rows:, :]
    new_values = ag[kv_heads + own_head, own_rows:, :]
    new_rows = ag.shape[1] - own_rows
    scores = lax.dot_general(own_q, new_keys, (((1,), (1,)), ((), ())), preferred_element_type=f32)
    scores = scores * score_scale
    row = lax.broadcasted_iota(jnp.int32, (own_rows, new_rows), 0)
    col = lax.broadcasted_iota(jnp.int32, (own_rows, new_rows), 1)
    row_bits, col_bits = half_rows.bit_length() - 1, drafts.bit_length() - 1
    same = lax.shift_right_logical(row, row_bits) == lax.shift_right_logical(col, col_bits)
    visible = same & ((col & (drafts - 1)) <= (row & (drafts - 1)))
    scores = jnp.where(visible, scores, floor_score)
    new_peak = jnp.max(scores, axis=-1, keepdims=True)
    new_weights = jnp.where(visible, jnp.exp(scores - new_peak), 0.0)
    new_total = jnp.sum(new_weights, axis=-1, keepdims=True)
    new_out = jnp.dot(new_weights.astype(bf16), new_values, preferred_element_type=f32)

    def wait_attention(step, source):
        st_copy(step, source, source).wait_recv()
        att_copy(step, source, source).wait_recv()

    each_peer(wait_attention)
    stats = jnp.concatenate(
        [st_recv[s] for s in range(n)] + [jnp.zeros((128 - n, 128), f32)], axis=0).T
    lane = lax.broadcasted_iota(jnp.int32, (own_rows, 128), 1)
    peaks = jnp.where(lane < n, stats[0:own_rows], floor_score)
    totals = stats[own_rows:2 * own_rows]
    top = jnp.maximum(jnp.max(peaks, axis=-1, keepdims=True), new_peak)
    factors = jnp.exp(peaks - top)
    new_factor = jnp.exp(new_peak - top)
    denominator = jnp.sum(factors * totals, axis=-1, keepdims=True) + new_factor * new_total
    numerator = new_factor * new_out
    for s in range(n):
        numerator = numerator + factors[:, s:s + 1] * a_recv[s].astype(f32)
    attended = numerator / denominator
    attention = jnp.concatenate(
        [jnp.concatenate(
            [attended[b * half_rows + h * drafts:b * half_rows + (h + 1) * drafts]
             for b in range(requests)], axis=0) for h in range(heads)], axis=1).astype(bf16)

    half_width = width // 2

    def out_part(i):
        out_copy(i).wait()
        part = jnp.dot(attention, o_buf[i], preferred_element_type=f32)
        return jnp.concatenate([part[:, :half_width], part[:, half_width:]], axis=0)

    def o_copy(step, target, source):
        return remote(OUT, o_send.at[step], o_recv.at[source], step, source, target)

    def send_out(step, target):
        o_send[step] = out_part(step - 1).astype(bf16)
        o_copy(step, target, me).start()

    each_peer(send_out)
    result = out_part(n - 1)

    def take_out(step, total):
        source = peer(step)
        o_copy(step, source, source).wait_recv()
        return total + o_recv[source].astype(f32)

    result = lax.fori_loop(1, n, take_out, result)
    result = jnp.concatenate([result[:tokens], result[tokens:]], axis=1).astype(bf16)
    for b in range(requests):
        out_ref[b] = result[b * drafts:(b + 1) * drafts]

    def finish(step, target):
        sq_copy(step, target, me).wait_send()
        ag_copy(step, target, me).wait_send()
        st_copy(step, target, me).wait_send()
        att_copy(step, target, me).wait_send()
        o_copy(step, target, me).wait_send()

    each_peer(finish)
    for j in range(chips):
        sib_copy(j).wait_send()
    for j in range(chips - 1):
        rs_copy(j).wait_send()


def fused_device(
    hidden, norm_gain, q_weight, kv_weight, out_weight, head_kind,
    ret_keys, ret_values, stream_keys, stream_values, cache_len, sink_len, window_len,
):
    n = lax.axis_size("seq")
    requests, drafts, width = hidden.shape
    tokens = requests * drafts
    head_dim = ret_keys.shape[3]
    own_width = out_weight.shape[0]
    own_rows = tokens * (own_width // head_dim)
    slots = ret_keys.shape[1] + stream_keys.shape[1]
    share = n // slots
    chips = n // 2
    piece = own_width + head_dim
    f32, bf16 = jnp.float32, jnp.bfloat16
    smem = pl.BlockSpec(memory_space=pltpu.SMEM)
    vmem = pl.BlockSpec(memory_space=pltpu.VMEM)
    hbm = pl.BlockSpec(memory_space=pltpu.HBM)
    scratch = [
        pltpu.VMEM((n, width, piece), bf16),
        pltpu.VMEM((n, own_width, width), bf16),
        pltpu.VMEM(ret_keys.shape, bf16),
        pltpu.VMEM(ret_values.shape, bf16),
        pltpu.VMEM(stream_keys.shape, bf16),
        pltpu.VMEM(stream_values.shape, bf16),
        pltpu.VMEM((1, 128), f32),
        pltpu.VMEM((n, 1, 128), f32),
        pltpu.VMEM((chips, tokens, piece), f32),
        pltpu.VMEM((chips, tokens, piece), f32),
        pltpu.VMEM((chips, tokens, piece), f32),
        pltpu.VMEM((chips, tokens, piece), f32),
        pltpu.VMEM((n, own_rows + 16, head_dim), bf16),
        pltpu.VMEM((slots, share, own_rows, head_dim), bf16),
        pltpu.VMEM((128, 128), f32),
        pltpu.VMEM((n, own_rows, head_dim), bf16),
        pltpu.VMEM((n, own_rows, head_dim), bf16),
        pltpu.VMEM((n, 1, 128), f32),
        pltpu.VMEM((n, 1, 128), f32),
        pltpu.VMEM((n, 2 * tokens, width // 2), bf16),
        pltpu.VMEM((n, 2 * tokens, width // 2), bf16),
        pltpu.SemaphoreType.DMA((3, n)),
        pltpu.SemaphoreType.DMA((2, 1 + requests)),
        pltpu.SemaphoreType.DMA((7, n)),
        pltpu.SemaphoreType.DMA((7, n)),
    ]
    return pl.pallas_call(
        step_kernel,
        out_shape=(
            jax.ShapeDtypeStruct(hidden.shape, bf16),
            jax.ShapeDtypeStruct((requests, drafts, kv_weight.shape[1]), bf16),
        ),
        in_specs=[smem] * 4 + [vmem] * 2 + [hbm] * 7,
        out_specs=(vmem, vmem),
        scratch_shapes=scratch,
        compiler_params=pltpu.CompilerParams(
            collective_id=0, has_side_effects=True, vmem_limit_bytes=52 * 2**20
        ),
        name="decode_step",
    )(
        head_kind, cache_len, sink_len, window_len, hidden, norm_gain.reshape(1, width),
        q_weight, kv_weight, out_weight, ret_keys, ret_values, stream_keys, stream_values,
    )


def power_of_two(value):
    return value & (value - 1) == 0


def fused_fits(
    hidden, norm_gain, q_weight, kv_weight, out_weight, head_kind,
    ret_keys, ret_values, stream_keys, stream_values, cache_len, sink_len, window_len,
):
    n = lax.axis_size("seq")
    requests, drafts, width = hidden.shape
    tokens = requests * drafts
    head_dim = ret_keys.shape[3]
    own_width = out_weight.shape[0]
    kv_heads = head_kind.shape[0]
    heads = own_width // head_dim
    return (
        n % 2 == 0 and n <= 128 and n % kv_heads == 0 and tokens == 8
        and head_dim == 128 and width % 256 == 0 and own_width % head_dim == 0
        and q_weight.shape[1] == n * own_width and kv_weight.shape[1] == n * head_dim
        and n == 2 * kv_heads and power_of_two(heads * drafts) and power_of_two(drafts)
        and heads * drafts % 16 == 0 and 2 * tokens * heads <= 128
        and ret_keys.shape[2] % 128 == 0 and stream_keys.shape[2] % 128 == 0
        and ret_keys.shape[1] + stream_keys.shape[1] == kv_heads
    )


def step_device(*args):
    return fused_device(*args) if fused_fits(*args) else per_device(*args)


def solution(mesh):
    in_specs = (
        P("groups", None, "seq"),
        P("seq"),
        P("seq", None),
        P("seq", None),
        P("seq", None),
        P(),
        P("groups", None, "seq", None),
        P("groups", None, "seq", None),
        P("groups", None, "seq", None),
        P("groups", None, "seq", None),
        P("groups"),
        P("groups"),
        P("groups"),
    )
    out_specs = (P("groups", None, "seq"), P("groups", None, None))
    return jax.shard_map(
        step_device, mesh=mesh, in_specs=in_specs, out_specs=out_specs, check_vma=False
    )
```

```python
import math

import jax
import jax.numpy as jnp
from jax import lax
from jax.experimental import pallas as pl
from jax.experimental.pallas import tpu as pltpu
from jax.sharding import PartitionSpec as P

SINK_CAP = 128
MESH = pl.DeviceIdType.MESH
GROUP = 4


epsilon = 1e-05
floor_score = -1e30


def joined(part, axis, combine):
    gathered = jax.tree.map(lambda a: lax.all_gather(a, axis), part)

    def take(source):
        return jax.tree.map(lambda a: lax.dynamic_index_in_dim(a, source, 0, False), gathered)

    return lax.fori_loop(
        1, lax.axis_size(axis), lambda source, state: combine(state, take(source)), take(0)
    )


def block_stats(queries, cache_keys, cache_values, visible, score_scale):
    scores = (
        jnp.einsum("bhqd,bhld->bhql", queries, cache_keys, preferred_element_type=jnp.float32)
        * score_scale
    )
    scores = jnp.where(visible, scores, floor_score)
    peak_score = jnp.max(scores, axis=-1)
    weights = jnp.where(visible, jnp.exp(scores - peak_score[..., None]), 0.0)
    weight_total = jnp.sum(weights, axis=-1)
    block_out = jnp.einsum(
        "bhql,bhld->bhqd",
        weights.astype(jnp.bfloat16),
        cache_values,
        preferred_element_type=jnp.float32,
    )
    return (peak_score, weight_total, block_out)


def spread_rows(values_in, selector):
    return jnp.einsum("brq,gr->bgq", values_in, selector, precision=lax.Precision.HIGHEST)


def spread_vectors(values_in, selector):
    return jnp.einsum("brqd,gr->bgqd", values_in, selector, precision=lax.Precision.HIGHEST)


def join_parts(first_part, second_part):
    top_score = jnp.maximum(first_part[0], second_part[0])
    left_factor = jnp.exp(first_part[0] - top_score)
    right_factor = jnp.exp(second_part[0] - top_score)
    joined_total = first_part[1] * left_factor + second_part[1] * right_factor
    joined_out = first_part[2] * left_factor[..., None] + second_part[2] * right_factor[..., None]
    return (top_score, joined_total, joined_out)


def per_device(
    hidden,
    norm_gain,
    q_weight,
    kv_weight,
    out_weight,
    head_kind,
    ret_keys,
    ret_values,
    stream_keys,
    stream_values,
    cache_len,
    sink_len,
    window_len,
):
    requests, drafts, local_width = hidden.shape
    kv_heads = head_kind.shape[0]
    head_dim = ret_keys.shape[3]
    retrieval = ret_keys.shape[1]
    running = stream_keys.shape[1]
    head_count = q_weight.shape[1] // head_dim
    group_size = head_count // kv_heads
    query_rows = drafts * group_size
    devices = lax.axis_size("seq")
    position = lax.axis_index("seq")
    tokens = requests * drafts
    hidden32 = hidden.astype(jnp.float32)
    squares = lax.psum(jnp.sum(hidden32 * hidden32, axis=-1), "seq")
    inverse = lax.rsqrt(squares / (local_width * devices) + epsilon)
    normed = (hidden32 * inverse[..., None] * norm_gain.astype(jnp.float32)).astype(jnp.bfloat16)
    flat_rows = normed.reshape(tokens, local_width)
    part_query = jnp.dot(flat_rows, q_weight, preferred_element_type=jnp.float32)
    part_fresh = jnp.dot(flat_rows, kv_weight, preferred_element_type=jnp.float32)
    whole_query, whole_fresh = lax.psum((part_query, part_fresh), "seq")
    queries = whole_query.astype(jnp.bfloat16)
    new_entries = whole_fresh.astype(jnp.bfloat16)
    grouped = (
        queries.reshape(requests, drafts, kv_heads, group_size, head_dim)
        .transpose(0, 2, 1, 3, 4)
        .reshape(requests, kv_heads, query_rows, head_dim)
    )
    fresh_split = new_entries.reshape(requests, drafts, 2, kv_heads, head_dim)
    new_keys = fresh_split[:, :, 0].transpose(0, 2, 1, 3)
    new_values = fresh_split[:, :, 1].transpose(0, 2, 1, 3)
    kind_flag = head_kind == 1
    rank_ret = jnp.cumsum(head_kind) - 1
    rank_str = jnp.cumsum(1 - head_kind) - 1
    select_ret = (
        kind_flag[:, None] & (rank_ret[:, None] == jnp.arange(retrieval)[None, :])
    ).astype(jnp.float32)
    select_str = (
        jnp.logical_not(kind_flag)[:, None] & (rank_str[:, None] == jnp.arange(running)[None, :])
    ).astype(jnp.float32)
    ret_queries = jnp.einsum(
        "bgqd,gr->brqd",
        grouped,
        select_ret.astype(jnp.bfloat16),
        preferred_element_type=jnp.float32,
    ).astype(jnp.bfloat16)
    str_queries = jnp.einsum(
        "bgqd,gr->brqd",
        grouped,
        select_str.astype(jnp.bfloat16),
        preferred_element_type=jnp.float32,
    ).astype(jnp.bfloat16)
    score_scale = head_dim ** (-0.5)
    cache_block = ret_keys.shape[2]
    cache_pos = position * cache_block + jnp.arange(cache_block)
    ret_visible = (cache_pos[None, :] < cache_len[:, None])[:, None, None, :]
    slot_block = stream_keys.shape[2]
    slot_pos = (position * slot_block + jnp.arange(slot_block))[None, :]
    sink_part = slot_pos < sink_len[:, None]
    recent_part = (slot_pos >= SINK_CAP) & (slot_pos < SINK_CAP + window_len[:, None])
    str_visible = (sink_part | recent_part)[:, None, None, :]
    ret_peak, ret_total, ret_out = block_stats(
        ret_queries, ret_keys, ret_values, ret_visible, score_scale
    )
    str_peak, str_total, str_out = block_stats(
        str_queries, stream_keys, stream_values, str_visible, score_scale
    )
    peak_all = spread_rows(ret_peak, select_ret) + spread_rows(str_peak, select_str)
    total_all = spread_rows(ret_total, select_ret) + spread_rows(str_total, select_str)
    out_all = spread_vectors(ret_out, select_ret) + spread_vectors(str_out, select_str)
    token_of_row = jnp.arange(query_rows) // group_size
    new_visible = jnp.arange(drafts)[None, :] <= token_of_row[:, None]
    new_peak, new_total, new_out = block_stats(
        grouped, new_keys, new_values, new_visible, score_scale
    )
    own_width = out_weight.shape[0]
    cache_peak, cache_total, cache_out = joined((peak_all, total_all, out_all), "seq", join_parts)
    top_score = jnp.maximum(cache_peak, new_peak)
    cache_factor = jnp.exp(cache_peak - top_score)
    new_factor = jnp.exp(new_peak - top_score)
    denominator = cache_total * cache_factor + new_total * new_factor
    attended = (
        cache_out * cache_factor[..., None] + new_out * new_factor[..., None]
    ) / denominator[..., None]
    attention = (
        attended.reshape(requests, kv_heads, drafts, group_size, head_dim)
        .transpose(0, 2, 1, 3, 4)
        .reshape(tokens, head_count * head_dim)
        .astype(jnp.bfloat16)
    )
    own_attention = lax.dynamic_slice_in_dim(attention, position * own_width, own_width, 1)
    own_output = lax.psum_scatter(
        lax.dot_general(
            out_weight, own_attention, (((0,), (1,)), ((), ())), preferred_element_type=jnp.float32
        ),
        "seq",
        scatter_dimension=0,
        tiled=True,
    )
    layer_output = own_output.T.reshape(requests, drafts, local_width).astype(jnp.bfloat16)
    return (layer_output, new_entries.reshape(requests, drafts, 2 * kv_heads * head_dim))


def step_kernel(
    kind_hbm, clen_hbm, slen_hbm, wlen_hbm, hidden_hbm, gain_hbm,
    qw_hbm, kvw_hbm, ow_hbm, rk_hbm, rv_hbm, sk_hbm, sv_hbm,
    out_ref, new_ref,
    kind_ref, clen_ref, slen_ref, wlen_ref, hidden_ref, gain_ref,
    w_buf, o_buf, rk, rv, sk, sv,
    sq_send, sq_recv, sib_send, sib_recv, rs_send, rs_recv, ag,
    a_res, stat_cols, a_send, a_recv, st_send, st_recv, o_send, o_recv,
    small_sem, load_sem, cache_sem, send_sem, recv_sem,
):
    f32, bf16 = jnp.float32, jnp.bfloat16
    n = lax.axis_size("seq")
    me = lax.axis_index("seq")
    core, chip, chips = lax.rem(me, 2), me // 2, n // 2
    sibling = me + 1 - 2 * core
    requests, drafts, width = hidden_ref.shape
    tokens = requests * drafts
    kv_heads = kind_ref.shape[0]
    retrieval, running = rk.shape[1], sk.shape[1]
    head_dim = rk.shape[3]
    own_width = o_buf.shape[1]
    piece = own_width + head_dim
    heads = own_width // head_dim
    share = n // kv_heads
    half_rows = heads * drafts
    own_rows = requests * half_rows
    group_rows = share * half_rows
    score_scale = head_dim ** (-0.5)
    exp_scale = score_scale * math.log2(math.e)
    SQ, SIB, RS, AG, ATT, STAT, OUT = range(7)

    def remote(kind, src, dst, send_slot, recv_slot, target):
        return pltpu.make_async_remote_copy(
            src_ref=src, dst_ref=dst,
            send_sem=send_sem.at[kind, send_slot], recv_sem=recv_sem.at[kind, recv_slot],
            device_id={"seq": target}, device_id_type=MESH,
        )

    def peer(step):
        return lax.rem(me + step, n)

    def each_peer(body):
        def run(step, carry):
            body(step, peer(step))
            return carry
        lax.fori_loop(1, n, run, 0)

    def chunk_owner(i):
        target_chip = lax.rem(chip + 1 + i % chips, chips)
        return 2 * target_chip + (1 - core if i < chips else core)

    def weight_copies(i):
        p = chunk_owner(i)
        qcols = pl.ds(pl.multiple_of(p * own_width, own_width), own_width)
        kcols = pl.ds(pl.multiple_of(p * head_dim, head_dim), head_dim)
        at = (i % GROUP) * piece
        return (
            pltpu.make_async_copy(
                qw_hbm.at[:, qcols], w_buf.at[i // GROUP, :, pl.ds(at, own_width)],
                load_sem.at[0, i]),
            pltpu.make_async_copy(
                kvw_hbm.at[:, kcols], w_buf.at[i // GROUP, :, pl.ds(at + own_width, head_dim)],
                load_sem.at[1, i]),
        )

    def out_copy(i):
        p = lax.rem(me + 1 + i, n)
        cols = pl.ds(pl.multiple_of(p * width, width), width)
        return pltpu.make_async_copy(
            ow_hbm.at[:, cols], o_buf.at[i // GROUP, :, pl.ds((i % GROUP) * width, width)],
            load_sem.at[2, i])

    small = [
        pltpu.make_async_copy(src, dst, small_sem.at[at]) for at, (src, dst) in enumerate((
            (hidden_hbm, hidden_ref), (gain_hbm, gain_ref), (kind_hbm, kind_ref),
            (clen_hbm, clen_ref), (slen_hbm, slen_ref), (wlen_hbm, wlen_ref)))
    ]
    for copy in small:
        copy.start()
    for i in range(n):
        for copy in weight_copies(i):
            copy.start()

    barrier = pltpu.get_barrier_semaphore()
    each_peer(lambda step, target: pl.semaphore_signal(
        barrier, inc=1, device_id={"seq": target}, device_id_type=MESH))

    for copy in small:
        copy.wait()
    hidden32 = jnp.concatenate([hidden_ref[b].astype(f32) for b in range(requests)], axis=0)
    squares = jnp.sum(hidden32 * hidden32, axis=-1, keepdims=True)
    eye = (lax.broadcasted_iota(jnp.int32, (tokens, 128), 0)
           == lax.broadcasted_iota(jnp.int32, (tokens, 128), 1))
    sq_send[...] = jnp.sum(jnp.where(eye, squares, 0.0), axis=0, keepdims=True)
    sq_recv[me] = sq_send[...]
    stat_cols[...] = jnp.zeros_like(stat_cols)
    pl.semaphore_wait(barrier, n - 1)

    def sq_copy(step, target, source):
        return remote(SQ, sq_send, sq_recv.at[source], step, source, target)

    each_peer(lambda step, target: sq_copy(step, target, me).start())

    cache_copies = [
        (pltpu.make_async_copy(sk_hbm, sk, cache_sem.at[0, 0]),
         pltpu.make_async_copy(sv_hbm, sv, cache_sem.at[1, 0])),
    ]
    for b in range(requests):
        cache_copies.append(
            (pltpu.make_async_copy(rk_hbm.at[b], rk.at[b], cache_sem.at[0, 1 + b]),
             pltpu.make_async_copy(rv_hbm.at[b], rv.at[b], cache_sem.at[1, 1 + b])))
    for pair in cache_copies:
        for copy in pair:
            copy.start()

    each_peer(lambda step, source: sq_copy(step, source, source).wait_recv())
    total_row = sq_recv[0]
    for s in range(1, n):
        total_row = total_row + sq_recv[s]
    total_sq = jnp.sum(jnp.where(eye, total_row, 0.0), axis=1, keepdims=True)
    inverse = lax.rsqrt(total_sq / (width * n) + epsilon)
    normed = (hidden32 * inverse * gain_ref[...].astype(f32).reshape(1, width)).astype(bf16)

    def project(group):
        for i in range(group * GROUP, (group + 1) * GROUP):
            for copy in weight_copies(i):
                copy.wait()
        whole = jnp.dot(normed, w_buf[group], preferred_element_type=f32)
        return [whole[:, at * piece:(at + 1) * piece] for at in range(GROUP)]

    def sib_copy(j):
        return remote(SIB, sib_send.at[j], sib_recv.at[j], j, j, sibling)

    for group in range(chips // GROUP):
        for at, value in enumerate(project(group)):
            sib_send[group * GROUP + at] = value
        for at in range(GROUP):
            sib_copy(group * GROUP + at).start()

    def rs_copy(j):
        target = 2 * lax.rem(chip + 1 + j, chips) + core
        return remote(RS, rs_send.at[j], rs_recv.at[j], j, j, target)

    for group in range(chips // GROUP):
        values = project(chips // GROUP + group)
        for at, value in enumerate(values):
            j = group * GROUP + at
            sib_copy(j).wait_recv()
            own = value + sib_recv[j]
            if j < chips - 1:
                rs_send[j] = own
                rs_copy(j).start()

    for i in range(n):
        out_copy(i).start()

    for j in range(chips - 1):
        rs_copy(j).wait_recv()
        own = own + rs_recv[j]

    def by_head(values):
        return jnp.concatenate(
            [values[b * drafts:(b + 1) * drafts, h * head_dim:(h + 1) * head_dim]
             for b in range(requests) for h in range(heads)], axis=0)

    packed = jnp.concatenate(
        [by_head(own[:, :own_width]), own[:, own_width:],
         jnp.zeros((ag.shape[2] - own_rows - tokens, head_dim), f32)], axis=0)
    ag[core, chip] = packed.astype(bf16)

    def ag_copy(step, target, source):
        return remote(
            AG, ag.at[core, source], ag.at[core, source], step, source, 2 * target + core)

    def each_chip(body):
        def run(step, carry):
            body(step, lax.rem(chip + step, chips))
            return carry
        lax.fori_loop(1, chips, run, 0)

    def pair_copy(side):
        return remote(AG, ag.at[side], ag.at[side], chips, chips, sibling)

    each_chip(lambda step, target: ag_copy(step, target, chip).start())

    kinds = [kind_ref[g] for g in range(kv_heads)]
    slot_of, before = [], 0
    for g in range(kv_heads):
        slot = jnp.where(kinds[g] == 1, before, retrieval + g - before)
        slot_of.append(jnp.minimum(slot, retrieval + running - 1))
        before = before + kinds[g]
    head_of = []
    for j in range(retrieval + running):
        found = 0
        for g in range(kv_heads):
            found = found + jnp.where(slot_of[g] == j, g, 0)
        head_of.append(jnp.minimum(found, kv_heads - 1))

    each_chip(lambda step, source: ag_copy(step, source, source).wait_recv())
    pair_copy(core).start()
    pair_copy(1 - core).wait_recv()

    for p in range(n):
        entries = ag[p % 2, p // 2, own_rows:, :]
        for b in range(requests):
            new_ref[b, :, p * head_dim:(p + 1) * head_dim] = entries[b * drafts:(b + 1) * drafts]

    def attend(b, j, keys, values, visible):
        q = jnp.concatenate(
            [ag[s % 2, head_of[j] * share // 2 + s // 2, b * half_rows:(b + 1) * half_rows, :]
             for s in range(share)], axis=0)
        scores = lax.dot_general(q, keys, (((1,), (1,)), ((), ())), preferred_element_type=f32)
        scores = jnp.where(visible, scores, floor_score)
        peak = jnp.max(scores, axis=-1, keepdims=True)
        weights = jnp.exp2((scores - peak) * exp_scale)
        total = jnp.sum(weights, axis=-1, keepdims=True)
        block = jnp.dot(weights.astype(bf16), values, preferred_element_type=f32)
        a_res[j, :, b * half_rows:(b + 1) * half_rows, :] = block.astype(bf16).reshape(
            share, half_rows, head_dim)
        lane = lax.broadcasted_iota(jnp.int32, (half_rows, 128), 1)
        for at, column in ((0, peak * score_scale), (own_rows, total)):
            rows = pl.ds(at + b * half_rows, half_rows)
            kept = stat_cols[rows, :]
            for s in range(share):
                kept = jnp.where(lane == share * head_of[j] + s,
                                 column[s * half_rows:(s + 1) * half_rows], kept)
            stat_cols[rows, :] = kept

    for copy in cache_copies[0]:
        copy.wait()
    slots = sk.shape[2]
    slot_pos = me * slots + lax.broadcasted_iota(jnp.int32, (1, slots), 1)
    positions = rk.shape[2]
    cache_pos = me * positions + lax.broadcasted_iota(jnp.int32, (1, positions), 1)
    for b in range(requests):
        seen = (slot_pos < slen_ref[b]) | (
            (slot_pos >= SINK_CAP) & (slot_pos < SINK_CAP + wlen_ref[b]))
        for r in range(running):
            attend(b, retrieval + r, sk[b, r], sv[b, r], seen)
    for b in range(requests):
        for copy in cache_copies[1 + b]:
            copy.wait()
        seen = cache_pos < clen_ref[b]
        for r in range(retrieval):
            attend(b, r, rk[b, r], rv[b, r], seen)

    stat_rows = stat_cols[...].T
    for p in range(n):
        st_send[p] = stat_rows[p:p + 1, :]
    for g in range(kv_heads):
        a_send[g * share:(g + 1) * share] = a_res[slot_of[g]]
    st_recv[me] = st_send[me]
    a_recv[me] = a_send[me]

    def att_copy(step, target, source):
        return remote(ATT, a_send.at[target], a_recv.at[source], step, source, target)

    def st_copy(step, target, source):
        return remote(STAT, st_send.at[target], st_recv.at[source], step, source, target)

    def send_attention(step, target):
        st_copy(step, target, me).start()
        att_copy(step, target, me).start()

    each_peer(send_attention)

    own_head = me // share
    own_q = ag[core, chip, 0:own_rows, :]
    new_keys = ag[lax.rem(own_head, 2), own_head // 2, own_rows:, :]
    new_values = ag[lax.rem(kv_heads + own_head, 2), (kv_heads + own_head) // 2, own_rows:, :]
    new_rows = ag.shape[2] - own_rows
    scores = lax.dot_general(own_q, new_keys, (((1,), (1,)), ((), ())), preferred_element_type=f32)
    scores = scores * score_scale
    row = lax.broadcasted_iota(jnp.int32, (own_rows, new_rows), 0)
    col = lax.broadcasted_iota(jnp.int32, (own_rows, new_rows), 1)
    row_bits, col_bits = half_rows.bit_length() - 1, drafts.bit_length() - 1
    same = lax.shift_right_logical(row, row_bits) == lax.shift_right_logical(col, col_bits)
    visible = same & ((col & (drafts - 1)) <= (row & (drafts - 1)))
    scores = jnp.where(visible, scores, floor_score)
    new_peak = jnp.max(scores, axis=-1, keepdims=True)
    new_weights = jnp.where(visible, jnp.exp(scores - new_peak), 0.0)
    new_total = jnp.sum(new_weights, axis=-1, keepdims=True)
    new_out = jnp.dot(new_weights.astype(bf16), new_values, preferred_element_type=f32)

    def wait_attention(step, source):
        st_copy(step, source, source).wait_recv()
        att_copy(step, source, source).wait_recv()

    each_peer(wait_attention)
    stats = jnp.concatenate(
        [st_recv[s] for s in range(n)] + [jnp.zeros((128 - n, 128), f32)], axis=0).T
    lane = lax.broadcasted_iota(jnp.int32, (own_rows, 128), 1)
    peaks = jnp.where(lane < n, stats[0:own_rows], floor_score)
    totals = stats[own_rows:2 * own_rows]
    top = jnp.maximum(jnp.max(peaks, axis=-1, keepdims=True), new_peak)
    factors = jnp.exp(peaks - top)
    new_factor = jnp.exp(new_peak - top)
    denominator = jnp.sum(factors * totals, axis=-1, keepdims=True) + new_factor * new_total
    numerator = new_factor * new_out
    for s in range(n):
        numerator = numerator + factors[:, s:s + 1] * a_recv[s].astype(f32)
    attended = numerator / denominator
    attention = jnp.concatenate(
        [jnp.concatenate(
            [attended[b * half_rows + h * drafts:b * half_rows + (h + 1) * drafts]
             for b in range(requests)], axis=0) for h in range(heads)], axis=1).astype(bf16)

    half_width = width // 2

    def o_copy(step, target, source):
        return remote(OUT, o_send.at[step], o_recv.at[source], step, source, target)

    for group in range(n // GROUP):
        for i in range(group * GROUP, (group + 1) * GROUP):
            out_copy(i).wait()
        whole = jnp.dot(attention, o_buf[group], preferred_element_type=f32)
        for at in range(GROUP):
            step = group * GROUP + at + 1
            begin = at * width
            result = jnp.concatenate(
                [whole[:, begin:begin + half_width], whole[:, begin + half_width:begin + width]],
                axis=0)
            if step < n:
                o_send[step] = result.astype(bf16)
                o_copy(step, peer(step), me).start()

    def take_out(step, total):
        source = peer(step)
        o_copy(step, source, source).wait_recv()
        return total + o_recv[source].astype(f32)

    result = lax.fori_loop(1, n, take_out, result)
    result = jnp.concatenate([result[:tokens], result[tokens:]], axis=1).astype(bf16)
    for b in range(requests):
        out_ref[b] = result[b * drafts:(b + 1) * drafts]

    def finish(step, target):
        sq_copy(step, target, me).wait_send()
        st_copy(step, target, me).wait_send()
        att_copy(step, target, me).wait_send()
        o_copy(step, target, me).wait_send()

    each_peer(finish)
    each_chip(lambda step, target: ag_copy(step, target, chip).wait_send())
    pair_copy(core).wait_send()
    for j in range(chips):
        sib_copy(j).wait_send()
    for j in range(chips - 1):
        rs_copy(j).wait_send()


def fused_device(
    hidden, norm_gain, q_weight, kv_weight, out_weight, head_kind,
    ret_keys, ret_values, stream_keys, stream_values, cache_len, sink_len, window_len,
):
    n = lax.axis_size("seq")
    requests, drafts, width = hidden.shape
    tokens = requests * drafts
    head_dim = ret_keys.shape[3]
    own_width = out_weight.shape[0]
    own_rows = tokens * (own_width // head_dim)
    slots = ret_keys.shape[1] + stream_keys.shape[1]
    share = n // slots
    chips = n // 2
    piece = own_width + head_dim
    f32, bf16 = jnp.float32, jnp.bfloat16
    vmem = pl.BlockSpec(memory_space=pltpu.VMEM)
    hbm = pl.BlockSpec(memory_space=pltpu.HBM)
    scratch = [
        pltpu.SMEM(head_kind.shape, jnp.int32),
        pltpu.SMEM(cache_len.shape, jnp.int32),
        pltpu.SMEM(sink_len.shape, jnp.int32),
        pltpu.SMEM(window_len.shape, jnp.int32),
        pltpu.VMEM(hidden.shape, bf16),
        pltpu.VMEM(norm_gain.shape, bf16),
        pltpu.VMEM((n // GROUP, width, GROUP * piece), bf16),
        pltpu.VMEM((n // GROUP, own_width, GROUP * width), bf16),
        pltpu.VMEM(ret_keys.shape, bf16),
        pltpu.VMEM(ret_values.shape, bf16),
        pltpu.VMEM(stream_keys.shape, bf16),
        pltpu.VMEM(stream_values.shape, bf16),
        pltpu.VMEM((1, 128), f32),
        pltpu.VMEM((n, 1, 128), f32),
        pltpu.VMEM((chips, tokens, piece), f32),
        pltpu.VMEM((chips, tokens, piece), f32),
        pltpu.VMEM((chips, tokens, piece), f32),
        pltpu.VMEM((chips, tokens, piece), f32),
        pltpu.VMEM((2, chips, own_rows + 16, head_dim), bf16),
        pltpu.VMEM((slots, share, own_rows, head_dim), bf16),
        pltpu.VMEM((128, 128), f32),
        pltpu.VMEM((n, own_rows, head_dim), bf16),
        pltpu.VMEM((n, own_rows, head_dim), bf16),
        pltpu.VMEM((n, 1, 128), f32),
        pltpu.VMEM((n, 1, 128), f32),
        pltpu.VMEM((n, 2 * tokens, width // 2), bf16),
        pltpu.VMEM((n, 2 * tokens, width // 2), bf16),
        pltpu.SemaphoreType.DMA((6,)),
        pltpu.SemaphoreType.DMA((3, n)),
        pltpu.SemaphoreType.DMA((2, 1 + requests)),
        pltpu.SemaphoreType.DMA((7, n)),
        pltpu.SemaphoreType.DMA((7, n)),
    ]
    return pl.pallas_call(
        step_kernel,
        out_shape=(
            jax.ShapeDtypeStruct(hidden.shape, bf16),
            jax.ShapeDtypeStruct((requests, drafts, kv_weight.shape[1]), bf16),
        ),
        in_specs=[hbm] * 13,
        out_specs=(vmem, vmem),
        scratch_shapes=scratch,
        compiler_params=pltpu.CompilerParams(
            collective_id=0, has_side_effects=True, vmem_limit_bytes=62 * 2**20
        ),
        name="decode_step",
    )(
        head_kind, cache_len, sink_len, window_len, hidden, norm_gain,
        q_weight, kv_weight, out_weight, ret_keys, ret_values, stream_keys, stream_values,
    )


def power_of_two(value):
    return value & (value - 1) == 0


def fused_fits(
    hidden, norm_gain, q_weight, kv_weight, out_weight, head_kind,
    ret_keys, ret_values, stream_keys, stream_values, cache_len, sink_len, window_len,
):
    n = lax.axis_size("seq")
    requests, drafts, width = hidden.shape
    tokens = requests * drafts
    head_dim = ret_keys.shape[3]
    own_width = out_weight.shape[0]
    kv_heads = head_kind.shape[0]
    heads = own_width // head_dim
    return (
        n % (2 * GROUP) == 0 and n <= 128 and n % kv_heads == 0 and tokens == 8
        and head_dim == 128 and width % 256 == 0 and own_width % head_dim == 0
        and q_weight.shape[1] == n * own_width and kv_weight.shape[1] == n * head_dim
        and n == 2 * kv_heads and power_of_two(heads * drafts) and power_of_two(drafts)
        and heads * drafts % 16 == 0 and 2 * tokens * heads <= 128
        and ret_keys.shape[2] % 128 == 0 and stream_keys.shape[2] % 128 == 0
        and ret_keys.shape[1] + stream_keys.shape[1] == kv_heads
    )


def step_device(*args):
    return fused_device(*args) if fused_fits(*args) else per_device(*args)


def solution(mesh):
    in_specs = (
        P("groups", None, "seq"),
        P("seq"),
        P("seq", None),
        P("seq", None),
        P("seq", None),
        P(),
        P("groups", None, "seq", None),
        P("groups", None, "seq", None),
        P("groups", None, "seq", None),
        P("groups", None, "seq", None),
        P("groups"),
        P("groups"),
        P("groups"),
    )
    out_specs = (P("groups", None, "seq"), P("groups", None, None))
    return jax.shard_map(
        step_device, mesh=mesh, in_specs=in_specs, out_specs=out_specs, check_vma=False
    )
```

```python
import math

import jax
import jax.numpy as jnp
from jax import lax
from jax.experimental import pallas as pl
from jax.experimental.pallas import tpu as pltpu
from jax.sharding import PartitionSpec as P

SINK_CAP = 128
MESH = pl.DeviceIdType.MESH
GROUP = 4


epsilon = 1e-05
floor_score = -1e30


def joined(part, axis, combine):
    gathered = jax.tree.map(lambda a: lax.all_gather(a, axis), part)

    def take(source):
        return jax.tree.map(lambda a: lax.dynamic_index_in_dim(a, source, 0, False), gathered)

    return lax.fori_loop(
        1, lax.axis_size(axis), lambda source, state: combine(state, take(source)), take(0)
    )


def block_stats(queries, cache_keys, cache_values, visible, score_scale):
    scores = (
        jnp.einsum("bhqd,bhld->bhql", queries, cache_keys, preferred_element_type=jnp.float32)
        * score_scale
    )
    scores = jnp.where(visible, scores, floor_score)
    peak_score = jnp.max(scores, axis=-1)
    weights = jnp.where(visible, jnp.exp(scores - peak_score[..., None]), 0.0)
    weight_total = jnp.sum(weights, axis=-1)
    block_out = jnp.einsum(
        "bhql,bhld->bhqd",
        weights.astype(jnp.bfloat16),
        cache_values,
        preferred_element_type=jnp.float32,
    )
    return (peak_score, weight_total, block_out)


def spread_rows(values_in, selector):
    return jnp.einsum("brq,gr->bgq", values_in, selector, precision=lax.Precision.HIGHEST)


def spread_vectors(values_in, selector):
    return jnp.einsum("brqd,gr->bgqd", values_in, selector, precision=lax.Precision.HIGHEST)


def join_parts(first_part, second_part):
    top_score = jnp.maximum(first_part[0], second_part[0])
    left_factor = jnp.exp(first_part[0] - top_score)
    right_factor = jnp.exp(second_part[0] - top_score)
    joined_total = first_part[1] * left_factor + second_part[1] * right_factor
    joined_out = first_part[2] * left_factor[..., None] + second_part[2] * right_factor[..., None]
    return (top_score, joined_total, joined_out)


def per_device(
    hidden,
    norm_gain,
    q_weight,
    kv_weight,
    out_weight,
    head_kind,
    ret_keys,
    ret_values,
    stream_keys,
    stream_values,
    cache_len,
    sink_len,
    window_len,
):
    requests, drafts, local_width = hidden.shape
    kv_heads = head_kind.shape[0]
    head_dim = ret_keys.shape[3]
    retrieval = ret_keys.shape[1]
    running = stream_keys.shape[1]
    head_count = q_weight.shape[1] // head_dim
    group_size = head_count // kv_heads
    query_rows = drafts * group_size
    devices = lax.axis_size("seq")
    position = lax.axis_index("seq")
    tokens = requests * drafts
    hidden32 = hidden.astype(jnp.float32)
    squares = lax.psum(jnp.sum(hidden32 * hidden32, axis=-1), "seq")
    inverse = lax.rsqrt(squares / (local_width * devices) + epsilon)
    normed = (hidden32 * inverse[..., None] * norm_gain.astype(jnp.float32)).astype(jnp.bfloat16)
    flat_rows = normed.reshape(tokens, local_width)
    part_query = jnp.dot(flat_rows, q_weight, preferred_element_type=jnp.float32)
    part_fresh = jnp.dot(flat_rows, kv_weight, preferred_element_type=jnp.float32)
    whole_query, whole_fresh = lax.psum((part_query, part_fresh), "seq")
    queries = whole_query.astype(jnp.bfloat16)
    new_entries = whole_fresh.astype(jnp.bfloat16)
    grouped = (
        queries.reshape(requests, drafts, kv_heads, group_size, head_dim)
        .transpose(0, 2, 1, 3, 4)
        .reshape(requests, kv_heads, query_rows, head_dim)
    )
    fresh_split = new_entries.reshape(requests, drafts, 2, kv_heads, head_dim)
    new_keys = fresh_split[:, :, 0].transpose(0, 2, 1, 3)
    new_values = fresh_split[:, :, 1].transpose(0, 2, 1, 3)
    kind_flag = head_kind == 1
    rank_ret = jnp.cumsum(head_kind) - 1
    rank_str = jnp.cumsum(1 - head_kind) - 1
    select_ret = (
        kind_flag[:, None] & (rank_ret[:, None] == jnp.arange(retrieval)[None, :])
    ).astype(jnp.float32)
    select_str = (
        jnp.logical_not(kind_flag)[:, None] & (rank_str[:, None] == jnp.arange(running)[None, :])
    ).astype(jnp.float32)
    ret_queries = jnp.einsum(
        "bgqd,gr->brqd",
        grouped,
        select_ret.astype(jnp.bfloat16),
        preferred_element_type=jnp.float32,
    ).astype(jnp.bfloat16)
    str_queries = jnp.einsum(
        "bgqd,gr->brqd",
        grouped,
        select_str.astype(jnp.bfloat16),
        preferred_element_type=jnp.float32,
    ).astype(jnp.bfloat16)
    score_scale = head_dim ** (-0.5)
    cache_block = ret_keys.shape[2]
    cache_pos = position * cache_block + jnp.arange(cache_block)
    ret_visible = (cache_pos[None, :] < cache_len[:, None])[:, None, None, :]
    slot_block = stream_keys.shape[2]
    slot_pos = (position * slot_block + jnp.arange(slot_block))[None, :]
    sink_part = slot_pos < sink_len[:, None]
    recent_part = (slot_pos >= SINK_CAP) & (slot_pos < SINK_CAP + window_len[:, None])
    str_visible = (sink_part | recent_part)[:, None, None, :]
    ret_peak, ret_total, ret_out = block_stats(
        ret_queries, ret_keys, ret_values, ret_visible, score_scale
    )
    str_peak, str_total, str_out = block_stats(
        str_queries, stream_keys, stream_values, str_visible, score_scale
    )
    peak_all = spread_rows(ret_peak, select_ret) + spread_rows(str_peak, select_str)
    total_all = spread_rows(ret_total, select_ret) + spread_rows(str_total, select_str)
    out_all = spread_vectors(ret_out, select_ret) + spread_vectors(str_out, select_str)
    token_of_row = jnp.arange(query_rows) // group_size
    new_visible = jnp.arange(drafts)[None, :] <= token_of_row[:, None]
    new_peak, new_total, new_out = block_stats(
        grouped, new_keys, new_values, new_visible, score_scale
    )
    own_width = out_weight.shape[0]
    cache_peak, cache_total, cache_out = joined((peak_all, total_all, out_all), "seq", join_parts)
    top_score = jnp.maximum(cache_peak, new_peak)
    cache_factor = jnp.exp(cache_peak - top_score)
    new_factor = jnp.exp(new_peak - top_score)
    denominator = cache_total * cache_factor + new_total * new_factor
    attended = (
        cache_out * cache_factor[..., None] + new_out * new_factor[..., None]
    ) / denominator[..., None]
    attention = (
        attended.reshape(requests, kv_heads, drafts, group_size, head_dim)
        .transpose(0, 2, 1, 3, 4)
        .reshape(tokens, head_count * head_dim)
        .astype(jnp.bfloat16)
    )
    own_attention = lax.dynamic_slice_in_dim(attention, position * own_width, own_width, 1)
    own_output = lax.psum_scatter(
        lax.dot_general(
            out_weight, own_attention, (((0,), (1,)), ((), ())), preferred_element_type=jnp.float32
        ),
        "seq",
        scatter_dimension=0,
        tiled=True,
    )
    layer_output = own_output.T.reshape(requests, drafts, local_width).astype(jnp.bfloat16)
    return (layer_output, new_entries.reshape(requests, drafts, 2 * kv_heads * head_dim))


def step_kernel(
    kind_hbm, clen_hbm, slen_hbm, wlen_hbm, hidden_hbm, gain_hbm,
    qw_hbm, kvw_hbm, ow_hbm, rk_hbm, rv_hbm, sk_hbm, sv_hbm,
    out_ref, new_ref,
    kind_ref, clen_ref, slen_ref, wlen_ref, hidden_ref, gain_ref,
    w_buf, o_buf, rk, rv, sk, sv,
    sq_send, sq_recv, sib_send, sib_recv, rs_send, rs_recv, ag,
    a_res, stat_cols, a_send, a_recv, st_send, st_recv, o_send, o_recv,
    small_sem, load_sem, cache_sem, send_sem, recv_sem,
):
    f32, bf16 = jnp.float32, jnp.bfloat16
    n = lax.axis_size("seq")
    me = lax.axis_index("seq")
    core, chip, chips = lax.rem(me, 2), me // 2, n // 2
    sibling = me + 1 - 2 * core
    requests, drafts, width = hidden_ref.shape
    tokens = requests * drafts
    kv_heads = kind_ref.shape[0]
    retrieval, running = rk.shape[1], sk.shape[1]
    head_dim = rk.shape[3]
    own_width = o_buf.shape[1]
    piece = own_width + head_dim
    heads = own_width // head_dim
    share = n // kv_heads
    half_rows = heads * drafts
    own_rows = requests * half_rows
    group_rows = share * half_rows
    score_scale = head_dim ** (-0.5)
    exp_scale = score_scale * math.log2(math.e)
    SQ, SIB, RS, AG, ATT, STAT, OUT = range(7)

    def remote(kind, src, dst, send_slot, recv_slot, target):
        return pltpu.make_async_remote_copy(
            src_ref=src, dst_ref=dst,
            send_sem=send_sem.at[kind, send_slot], recv_sem=recv_sem.at[kind, recv_slot],
            device_id={"seq": target}, device_id_type=MESH,
        )

    def peer(step):
        return lax.rem(me + step, n)

    def each_peer(body):
        for step in range(1, n):
            body(step, peer(step))

    def arrived(buffer, sem):
        span = buffer.at[pl.ds(1, n - 1)]
        pltpu.make_async_copy(span, span, sem).wait()

    slabs = n // GROUP
    own_slab = me // GROUP

    def slab(k):
        return lax.rem(own_slab + 1 + k, slabs)

    def columns(k, size):
        return pl.ds(pl.multiple_of(slab(k) * (GROUP * size), GROUP * size), GROUP * size)

    def weight_copies(k):
        return (
            pltpu.make_async_copy(
                qw_hbm.at[:, columns(k, own_width)],
                w_buf.at[k, :, pl.ds(0, GROUP * own_width)], load_sem.at[0, k]),
            pltpu.make_async_copy(
                kvw_hbm.at[:, columns(k, head_dim)],
                w_buf.at[k, :, pl.ds(GROUP * own_width, GROUP * head_dim)], load_sem.at[1, k]),
        )

    def out_copy(k):
        return pltpu.make_async_copy(
            ow_hbm.at[:, columns(k, width)], o_buf.at[k], load_sem.at[2, k])

    small = [
        pltpu.make_async_copy(src, dst, small_sem.at[at]) for at, (src, dst) in enumerate((
            (hidden_hbm, hidden_ref), (gain_hbm, gain_ref), (kind_hbm, kind_ref),
            (clen_hbm, clen_ref), (slen_hbm, slen_ref), (wlen_hbm, wlen_ref)))
    ]
    for copy in small:
        copy.start()
    barrier = pltpu.get_barrier_semaphore()
    each_peer(lambda step, target: pl.semaphore_signal(
        barrier, inc=1, device_id={"seq": target}, device_id_type=MESH))
    for k in range(slabs):
        for copy in weight_copies(k):
            copy.start()

    for copy in small:
        copy.wait()
    hidden32 = jnp.concatenate([hidden_ref[b].astype(f32) for b in range(requests)], axis=0)
    squares = jnp.sum(hidden32 * hidden32, axis=-1, keepdims=True)
    eye = (lax.broadcasted_iota(jnp.int32, (tokens, 128), 0)
           == lax.broadcasted_iota(jnp.int32, (tokens, 128), 1))
    sq_send[...] = jnp.sum(jnp.where(eye, squares, 0.0), axis=0, keepdims=True)
    sq_recv[0] = sq_send[...]
    stat_cols[...] = jnp.zeros_like(stat_cols)
    pl.semaphore_wait(barrier, n - 1)

    def sq_copy(step, target):
        return remote(SQ, sq_send, sq_recv.at[step], 0, 0, target)

    each_peer(lambda step, target: sq_copy(step, target).start())

    cache_copies = [
        (pltpu.make_async_copy(sk_hbm, sk, cache_sem.at[0, 0]),
         pltpu.make_async_copy(sv_hbm, sv, cache_sem.at[1, 0])),
    ]
    for b in range(requests):
        cache_copies.append(
            (pltpu.make_async_copy(rk_hbm.at[b], rk.at[b], cache_sem.at[0, 1 + b]),
             pltpu.make_async_copy(rv_hbm.at[b], rv.at[b], cache_sem.at[1, 1 + b])))
    for pair in cache_copies:
        for copy in pair:
            copy.start()

    arrived(sq_recv, recv_sem.at[SQ, 0])
    total_row = sq_recv[0]
    for s in range(1, n):
        total_row = total_row + sq_recv[s]
    total_sq = jnp.sum(jnp.where(eye, total_row, 0.0), axis=1, keepdims=True)
    inverse = lax.rsqrt(total_sq / (width * n) + epsilon)
    normed = (hidden32 * inverse * gain_ref[...].astype(f32).reshape(1, width)).astype(bf16)

    def part(whole, owner):
        return jnp.concatenate(
            [whole[:, owner * own_width:(owner + 1) * own_width],
             whole[:, GROUP * own_width + owner * head_dim:
                   GROUP * own_width + (owner + 1) * head_dim]], axis=1)

    def pick(flag, first, second):
        return jnp.where(flag == 0, first, second)

    def sib_copy(k):
        return remote(SIB, sib_send.at[k], sib_recv.at[k], k, k, sibling)

    pairs = GROUP // 2
    own_pair = lax.rem(chip, pairs)

    def rs_copy(k, u):
        target = 2 * (slab(k) * pairs + u) + core
        return remote(
            RS, rs_send.at[k * pairs + u], rs_recv.at[k * pairs + own_pair],
            k * pairs + u, k * pairs + own_pair, target)

    def rs_arrival(k, u):
        return remote(
            RS, rs_send.at[0], rs_recv.at[k * pairs + u], 0, k * pairs + u, sibling)

    mine = []

    def send_sums(k):
        sib_copy(k).wait_recv()
        for u in range(pairs):
            rs_send[k * pairs + u] = mine[k][u] + sib_recv[k, u]
            rs_copy(k, u).start()

    for k in range(slabs):
        for copy in weight_copies(k):
            copy.wait()
        whole = jnp.dot(normed, w_buf[k], preferred_element_type=f32)
        sides = [(part(whole, 2 * u), part(whole, 2 * u + 1)) for u in range(pairs)]
        mine.append([pick(core, *side) for side in sides])
        for u in range(pairs):
            sib_send[k, u] = pick(core, sides[u][1], sides[u][0])
        sib_copy(k).start()
        if k > 0:
            send_sums(k - 1)

    last = slabs - 1
    sib_copy(last).wait_recv()
    for u in range(pairs):
        rs_send[last * pairs + u] = mine[last][u] + sib_recv[last, u]
    for hop in range(1, pairs):
        rs_copy(last, lax.rem(own_pair + hop, pairs)).start()
    own = rs_send[last * pairs + own_pair]

    for k in range(slabs):
        out_copy(k).start()

    for k in range(last):
        for u in range(pairs):
            rs_arrival(k, u).wait_recv()
            own = own + rs_recv[k * pairs + u]
    for hop in range(1, pairs):
        u = lax.rem(own_pair + hop, pairs)
        rs_arrival(last, u).wait_recv()
        own = own + rs_recv[last * pairs + u]

    def by_head(values):
        return jnp.concatenate(
            [values[b * drafts:(b + 1) * drafts, h * head_dim:(h + 1) * head_dim]
             for b in range(requests) for h in range(heads)], axis=0)

    packed = jnp.concatenate(
        [by_head(own[:, :own_width]), own[:, own_width:],
         jnp.zeros((ag.shape[2] - own_rows - tokens, head_dim), f32)], axis=0)
    ag[core, chip] = packed.astype(bf16)

    def ag_copy(step, target, source):
        return remote(
            AG, ag.at[core, source], ag.at[core, source], step, source, 2 * target + core)

    def each_chip(body):
        for step in range(1, chips):
            body(step, lax.rem(chip + step, chips))

    def pair_copy(side):
        return remote(AG, ag.at[side], ag.at[side], chips, chips, sibling)

    each_chip(lambda step, target: ag_copy(step, target, chip).start())

    kinds = [kind_ref[g] for g in range(kv_heads)]
    slot_of, before = [], 0
    for g in range(kv_heads):
        slot = jnp.where(kinds[g] == 1, before, retrieval + g - before)
        slot_of.append(jnp.minimum(slot, retrieval + running - 1))
        before = before + kinds[g]
    head_of = []
    for j in range(retrieval + running):
        found = 0
        for g in range(kv_heads):
            found = found + jnp.where(slot_of[g] == j, g, 0)
        head_of.append(jnp.minimum(found, kv_heads - 1))

    each_chip(lambda step, source: ag_copy(step, source, source).wait_recv())
    pair_copy(core).start()
    pair_copy(1 - core).wait_recv()

    for p in range(n):
        entries = ag[p % 2, p // 2, own_rows:, :]
        for b in range(requests):
            new_ref[b, :, p * head_dim:(p + 1) * head_dim] = entries[b * drafts:(b + 1) * drafts]

    def score(b, j, keys):
        q = jnp.concatenate(
            [ag[s % 2, head_of[j] * share // 2 + s // 2, b * half_rows:(b + 1) * half_rows, :]
             for s in range(share)], axis=0)
        return lax.dot_general(q, keys, (((1,), (1,)), ((), ())), preferred_element_type=f32)

    def attend(b, j, scores, values, visible):
        scores = jnp.where(visible, scores, floor_score)
        peak = jnp.max(scores, axis=-1, keepdims=True)
        weights = jnp.exp2((scores - peak) * exp_scale)
        total = jnp.sum(weights, axis=-1, keepdims=True)
        block = jnp.dot(weights.astype(bf16), values, preferred_element_type=f32)
        a_res[j, :, b * half_rows:(b + 1) * half_rows, :] = block.astype(bf16).reshape(
            share, half_rows, head_dim)
        lane = lax.broadcasted_iota(jnp.int32, (half_rows, 128), 1)
        for at, column in ((0, peak * score_scale), (own_rows, total)):
            rows = pl.ds(at + b * half_rows, half_rows)
            kept = stat_cols[rows, :]
            for s in range(share):
                kept = jnp.where(lane == share * head_of[j] + s,
                                 column[s * half_rows:(s + 1) * half_rows], kept)
            stat_cols[rows, :] = kept

    for copy in cache_copies[0]:
        copy.wait()
    slots = sk.shape[2]
    slot_pos = me * slots + lax.broadcasted_iota(jnp.int32, (1, slots), 1)
    positions = rk.shape[2]
    cache_pos = me * positions + lax.broadcasted_iota(jnp.int32, (1, positions), 1)
    for b in range(requests):
        seen = (slot_pos < slen_ref[b]) | (
            (slot_pos >= SINK_CAP) & (slot_pos < SINK_CAP + wlen_ref[b]))
        later = score(b, retrieval, sk[b, 0])
        for r in range(running):
            scores = later
            if r + 1 < running:
                later = score(b, retrieval + r + 1, sk[b, r + 1])
            attend(b, retrieval + r, scores, sv[b, r], seen)
    for b in range(requests):
        for copy in cache_copies[1 + b]:
            copy.wait()
        seen = cache_pos < clen_ref[b]
        later = score(b, 0, rk[b, 0])
        for r in range(retrieval):
            scores = later
            if r + 1 < retrieval:
                later = score(b, r + 1, rk[b, r + 1])
            attend(b, r, scores, rv[b, r], seen)

    stat_rows = stat_cols[...].T
    for p in range(n):
        st_send[p] = stat_rows[p:p + 1, :]
    for g in range(kv_heads):
        a_send[g * share:(g + 1) * share] = a_res[slot_of[g]]
    st_recv[0] = st_send[me]
    a_recv[0] = a_send[me]

    def att_copy(step, target):
        return remote(ATT, a_send.at[target], a_recv.at[step], 0, 0, target)

    def st_copy(step, target):
        return remote(STAT, st_send.at[target], st_recv.at[step], 0, 0, target)

    each_peer(lambda step, target: st_copy(step, target).start())
    each_peer(lambda step, target: att_copy(step, target).start())

    own_head = me // share
    own_q = ag[core, chip, 0:own_rows, :]
    new_keys = ag[lax.rem(own_head, 2), own_head // 2, own_rows:, :]
    new_values = ag[lax.rem(kv_heads + own_head, 2), (kv_heads + own_head) // 2, own_rows:, :]
    new_rows = ag.shape[2] - own_rows
    scores = lax.dot_general(own_q, new_keys, (((1,), (1,)), ((), ())), preferred_element_type=f32)
    scores = scores * score_scale
    row = lax.broadcasted_iota(jnp.int32, (own_rows, new_rows), 0)
    col = lax.broadcasted_iota(jnp.int32, (own_rows, new_rows), 1)
    row_bits, col_bits = half_rows.bit_length() - 1, drafts.bit_length() - 1
    same = lax.shift_right_logical(row, row_bits) == lax.shift_right_logical(col, col_bits)
    visible = same & ((col & (drafts - 1)) <= (row & (drafts - 1)))
    scores = jnp.where(visible, scores, floor_score)
    new_peak = jnp.max(scores, axis=-1, keepdims=True)
    new_weights = jnp.where(visible, jnp.exp(scores - new_peak), 0.0)
    new_total = jnp.sum(new_weights, axis=-1, keepdims=True)
    new_out = jnp.dot(new_weights.astype(bf16), new_values, preferred_element_type=f32)

    arrived(st_recv, recv_sem.at[STAT, 0])
    stats = jnp.concatenate(
        [st_recv[s] for s in range(n)] + [jnp.zeros((128 - n, 128), f32)], axis=0).T
    lane = lax.broadcasted_iota(jnp.int32, (own_rows, 128), 1)
    peaks = jnp.where(lane < n, stats[0:own_rows], floor_score)
    totals = stats[own_rows:2 * own_rows]
    top = jnp.maximum(jnp.max(peaks, axis=-1, keepdims=True), new_peak)
    factors = jnp.exp(peaks - top)
    new_factor = jnp.exp(new_peak - top)
    denominator = jnp.sum(factors * totals, axis=-1, keepdims=True) + new_factor * new_total
    numerator = new_factor * new_out
    arrived(a_recv, recv_sem.at[ATT, 0])
    for s in range(n):
        numerator = numerator + factors[:, s:s + 1] * a_recv[s].astype(f32)
    attended = numerator / denominator
    attention = jnp.concatenate(
        [jnp.concatenate(
            [attended[b * half_rows + h * drafts:b * half_rows + (h + 1) * drafts]
             for b in range(requests)], axis=0) for h in range(heads)], axis=1).astype(bf16)

    half_width = width // 2

    def o_copy(k, at):
        owner = slab(k) * GROUP + at
        slot = k * GROUP + lax.rem(me, GROUP)
        return remote(OUT, o_send.at[k * GROUP + at], o_recv.at[slot], k * GROUP + at, slot, owner)

    def o_arrival(k, at):
        slot = k * GROUP + at
        return remote(OUT, o_send.at[0], o_recv.at[slot], 0, slot, sibling)

    own_at = lax.rem(me, GROUP)
    for k in range(slabs):
        out_copy(k).wait()
        whole = jnp.dot(attention, o_buf[k], preferred_element_type=f32)
        for at in range(GROUP):
            begin = at * width
            o_send[k * GROUP + at] = jnp.concatenate(
                [whole[:, begin:begin + half_width], whole[:, begin + half_width:begin + width]],
                axis=0).astype(bf16)
            if k < slabs - 1:
                o_copy(k, at).start()
    for hop in range(1, GROUP):
        o_copy(slabs - 1, lax.rem(own_at + hop, GROUP)).start()
    result = o_send[(slabs - 1) * GROUP + own_at].astype(f32)
    for k in range(slabs):
        for at in range(GROUP):
            if k < slabs - 1:
                o_arrival(k, at).wait_recv()
                result = result + o_recv[k * GROUP + at].astype(f32)
            elif at > 0:
                place = lax.rem(own_at + at, GROUP)
                o_arrival(k, place).wait_recv()
                result = result + o_recv[k * GROUP + place].astype(f32)
    result = jnp.concatenate([result[:tokens], result[tokens:]], axis=1).astype(bf16)
    for b in range(requests):
        out_ref[b] = result[b * drafts:(b + 1) * drafts]

    arrived(sq_recv, send_sem.at[SQ, 0])
    arrived(st_recv, send_sem.at[STAT, 0])
    arrived(a_recv, send_sem.at[ATT, 0])
    each_chip(lambda step, target: ag_copy(step, target, chip).wait_send())
    pair_copy(core).wait_send()
    for k in range(slabs):
        sib_copy(k).wait_send()
        if k < last:
            for u in range(pairs):
                rs_copy(k, u).wait_send()
            for at in range(GROUP):
                o_copy(k, at).wait_send()
    for hop in range(1, pairs):
        rs_copy(last, lax.rem(own_pair + hop, pairs)).wait_send()
    for hop in range(1, GROUP):
        o_copy(last, lax.rem(own_at + hop, GROUP)).wait_send()


def fused_device(
    hidden, norm_gain, q_weight, kv_weight, out_weight, head_kind,
    ret_keys, ret_values, stream_keys, stream_values, cache_len, sink_len, window_len,
):
    n = lax.axis_size("seq")
    requests, drafts, width = hidden.shape
    tokens = requests * drafts
    head_dim = ret_keys.shape[3]
    own_width = out_weight.shape[0]
    own_rows = tokens * (own_width // head_dim)
    slots = ret_keys.shape[1] + stream_keys.shape[1]
    share = n // slots
    chips = n // 2
    piece = own_width + head_dim
    f32, bf16 = jnp.float32, jnp.bfloat16
    vmem = pl.BlockSpec(memory_space=pltpu.VMEM)
    hbm = pl.BlockSpec(memory_space=pltpu.HBM)
    scratch = [
        pltpu.SMEM(head_kind.shape, jnp.int32),
        pltpu.SMEM(cache_len.shape, jnp.int32),
        pltpu.SMEM(sink_len.shape, jnp.int32),
        pltpu.SMEM(window_len.shape, jnp.int32),
        pltpu.VMEM(hidden.shape, bf16),
        pltpu.VMEM(norm_gain.shape, bf16),
        pltpu.VMEM((n // GROUP, width, GROUP * piece), bf16),
        pltpu.VMEM((n // GROUP, own_width, GROUP * width), bf16),
        pltpu.VMEM(ret_keys.shape, bf16),
        pltpu.VMEM(ret_values.shape, bf16),
        pltpu.VMEM(stream_keys.shape, bf16),
        pltpu.VMEM(stream_values.shape, bf16),
        pltpu.VMEM((1, 128), f32),
        pltpu.VMEM((n, 1, 128), f32),
        pltpu.VMEM((n // GROUP, GROUP // 2, tokens, piece), f32),
        pltpu.VMEM((n // GROUP, GROUP // 2, tokens, piece), f32),
        pltpu.VMEM((chips, tokens, piece), f32),
        pltpu.VMEM((chips, tokens, piece), f32),
        pltpu.VMEM((2, chips, own_rows + 16, head_dim), bf16),
        pltpu.VMEM((slots, share, own_rows, head_dim), bf16),
        pltpu.VMEM((128, 128), f32),
        pltpu.VMEM((n, own_rows, head_dim), bf16),
        pltpu.VMEM((n, own_rows, head_dim), bf16),
        pltpu.VMEM((n, 1, 128), f32),
        pltpu.VMEM((n, 1, 128), f32),
        pltpu.VMEM((n, 2 * tokens, width // 2), bf16),
        pltpu.VMEM((n, 2 * tokens, width // 2), bf16),
        pltpu.SemaphoreType.DMA((6,)),
        pltpu.SemaphoreType.DMA((3, n)),
        pltpu.SemaphoreType.DMA((2, 1 + requests)),
        pltpu.SemaphoreType.DMA((7, n)),
        pltpu.SemaphoreType.DMA((7, n)),
    ]
    return pl.pallas_call(
        step_kernel,
        out_shape=(
            jax.ShapeDtypeStruct(hidden.shape, bf16),
            jax.ShapeDtypeStruct((requests, drafts, kv_weight.shape[1]), bf16),
        ),
        in_specs=[hbm] * 13,
        out_specs=(vmem, vmem),
        scratch_shapes=scratch,
        compiler_params=pltpu.CompilerParams(
            collective_id=0, has_side_effects=True, vmem_limit_bytes=62 * 2**20
        ),
        name="decode_step",
    )(
        head_kind, cache_len, sink_len, window_len, hidden, norm_gain,
        q_weight, kv_weight, out_weight, ret_keys, ret_values, stream_keys, stream_values,
    )


def power_of_two(value):
    return value & (value - 1) == 0


def fused_fits(
    hidden, norm_gain, q_weight, kv_weight, out_weight, head_kind,
    ret_keys, ret_values, stream_keys, stream_values, cache_len, sink_len, window_len,
):
    n = lax.axis_size("seq")
    requests, drafts, width = hidden.shape
    tokens = requests * drafts
    head_dim = ret_keys.shape[3]
    own_width = out_weight.shape[0]
    kv_heads = head_kind.shape[0]
    heads = own_width // head_dim
    return (
        n % (2 * GROUP) == 0 and n <= 128 and n % kv_heads == 0 and tokens == 8
        and head_dim == 128 and width % 256 == 0 and own_width % head_dim == 0
        and q_weight.shape[1] == n * own_width and kv_weight.shape[1] == n * head_dim
        and n == 2 * kv_heads and power_of_two(heads * drafts) and power_of_two(drafts)
        and heads * drafts % 16 == 0 and 2 * tokens * heads <= 128
        and ret_keys.shape[2] % 128 == 0 and stream_keys.shape[2] % 128 == 0
        and ret_keys.shape[1] + stream_keys.shape[1] == kv_heads
    )


def step_device(*args):
    return fused_device(*args) if fused_fits(*args) else per_device(*args)


def solution(mesh):
    in_specs = (
        P("groups", None, "seq"),
        P("seq"),
        P("seq", None),
        P("seq", None),
        P("seq", None),
        P(),
        P("groups", None, "seq", None),
        P("groups", None, "seq", None),
        P("groups", None, "seq", None),
        P("groups", None, "seq", None),
        P("groups"),
        P("groups"),
        P("groups"),
    )
    out_specs = (P("groups", None, "seq"), P("groups", None, None))
    return jax.shard_map(
        step_device, mesh=mesh, in_specs=in_specs, out_specs=out_specs, check_vma=False
    )
```

```python
import math

import jax
import jax.numpy as jnp
from jax import lax
from jax.experimental import pallas as pl
from jax.experimental.pallas import tpu as pltpu
from jax.sharding import PartitionSpec as P

SINK_CAP = 128
MESH = pl.DeviceIdType.MESH
GROUP = 4


epsilon = 1e-05
floor_score = -1e30


def joined(part, axis, combine):
    gathered = jax.tree.map(lambda a: lax.all_gather(a, axis), part)

    def take(source):
        return jax.tree.map(lambda a: lax.dynamic_index_in_dim(a, source, 0, False), gathered)

    return lax.fori_loop(
        1, lax.axis_size(axis), lambda source, state: combine(state, take(source)), take(0)
    )


def block_stats(queries, cache_keys, cache_values, visible, score_scale):
    scores = (
        jnp.einsum("bhqd,bhld->bhql", queries, cache_keys, preferred_element_type=jnp.float32)
        * score_scale
    )
    scores = jnp.where(visible, scores, floor_score)
    peak_score = jnp.max(scores, axis=-1)
    weights = jnp.where(visible, jnp.exp(scores - peak_score[..., None]), 0.0)
    weight_total = jnp.sum(weights, axis=-1)
    block_out = jnp.einsum(
        "bhql,bhld->bhqd",
        weights.astype(jnp.bfloat16),
        cache_values,
        preferred_element_type=jnp.float32,
    )
    return (peak_score, weight_total, block_out)


def spread_rows(values_in, selector):
    return jnp.einsum("brq,gr->bgq", values_in, selector, precision=lax.Precision.HIGHEST)


def spread_vectors(values_in, selector):
    return jnp.einsum("brqd,gr->bgqd", values_in, selector, precision=lax.Precision.HIGHEST)


def join_parts(first_part, second_part):
    top_score = jnp.maximum(first_part[0], second_part[0])
    left_factor = jnp.exp(first_part[0] - top_score)
    right_factor = jnp.exp(second_part[0] - top_score)
    joined_total = first_part[1] * left_factor + second_part[1] * right_factor
    joined_out = first_part[2] * left_factor[..., None] + second_part[2] * right_factor[..., None]
    return (top_score, joined_total, joined_out)


def per_device(
    hidden,
    norm_gain,
    q_weight,
    kv_weight,
    out_weight,
    head_kind,
    ret_keys,
    ret_values,
    stream_keys,
    stream_values,
    cache_len,
    sink_len,
    window_len,
):
    requests, drafts, local_width = hidden.shape
    kv_heads = head_kind.shape[0]
    head_dim = ret_keys.shape[3]
    retrieval = ret_keys.shape[1]
    running = stream_keys.shape[1]
    head_count = q_weight.shape[1] // head_dim
    group_size = head_count // kv_heads
    query_rows = drafts * group_size
    devices = lax.axis_size("seq")
    position = lax.axis_index("seq")
    tokens = requests * drafts
    hidden32 = hidden.astype(jnp.float32)
    squares = lax.psum(jnp.sum(hidden32 * hidden32, axis=-1), "seq")
    inverse = lax.rsqrt(squares / (local_width * devices) + epsilon)
    normed = (hidden32 * inverse[..., None] * norm_gain.astype(jnp.float32)).astype(jnp.bfloat16)
    flat_rows = normed.reshape(tokens, local_width)
    part_query = jnp.dot(flat_rows, q_weight, preferred_element_type=jnp.float32)
    part_fresh = jnp.dot(flat_rows, kv_weight, preferred_element_type=jnp.float32)
    whole_query, whole_fresh = lax.psum((part_query, part_fresh), "seq")
    queries = whole_query.astype(jnp.bfloat16)
    new_entries = whole_fresh.astype(jnp.bfloat16)
    grouped = (
        queries.reshape(requests, drafts, kv_heads, group_size, head_dim)
        .transpose(0, 2, 1, 3, 4)
        .reshape(requests, kv_heads, query_rows, head_dim)
    )
    fresh_split = new_entries.reshape(requests, drafts, 2, kv_heads, head_dim)
    new_keys = fresh_split[:, :, 0].transpose(0, 2, 1, 3)
    new_values = fresh_split[:, :, 1].transpose(0, 2, 1, 3)
    kind_flag = head_kind == 1
    rank_ret = jnp.cumsum(head_kind) - 1
    rank_str = jnp.cumsum(1 - head_kind) - 1
    select_ret = (
        kind_flag[:, None] & (rank_ret[:, None] == jnp.arange(retrieval)[None, :])
    ).astype(jnp.float32)
    select_str = (
        jnp.logical_not(kind_flag)[:, None] & (rank_str[:, None] == jnp.arange(running)[None, :])
    ).astype(jnp.float32)
    ret_queries = jnp.einsum(
        "bgqd,gr->brqd",
        grouped,
        select_ret.astype(jnp.bfloat16),
        preferred_element_type=jnp.float32,
    ).astype(jnp.bfloat16)
    str_queries = jnp.einsum(
        "bgqd,gr->brqd",
        grouped,
        select_str.astype(jnp.bfloat16),
        preferred_element_type=jnp.float32,
    ).astype(jnp.bfloat16)
    score_scale = head_dim ** (-0.5)
    cache_block = ret_keys.shape[2]
    cache_pos = position * cache_block + jnp.arange(cache_block)
    ret_visible = (cache_pos[None, :] < cache_len[:, None])[:, None, None, :]
    slot_block = stream_keys.shape[2]
    slot_pos = (position * slot_block + jnp.arange(slot_block))[None, :]
    sink_part = slot_pos < sink_len[:, None]
    recent_part = (slot_pos >= SINK_CAP) & (slot_pos < SINK_CAP + window_len[:, None])
    str_visible = (sink_part | recent_part)[:, None, None, :]
    ret_peak, ret_total, ret_out = block_stats(
        ret_queries, ret_keys, ret_values, ret_visible, score_scale
    )
    str_peak, str_total, str_out = block_stats(
        str_queries, stream_keys, stream_values, str_visible, score_scale
    )
    peak_all = spread_rows(ret_peak, select_ret) + spread_rows(str_peak, select_str)
    total_all = spread_rows(ret_total, select_ret) + spread_rows(str_total, select_str)
    out_all = spread_vectors(ret_out, select_ret) + spread_vectors(str_out, select_str)
    token_of_row = jnp.arange(query_rows) // group_size
    new_visible = jnp.arange(drafts)[None, :] <= token_of_row[:, None]
    new_peak, new_total, new_out = block_stats(
        grouped, new_keys, new_values, new_visible, score_scale
    )
    own_width = out_weight.shape[0]
    cache_peak, cache_total, cache_out = joined((peak_all, total_all, out_all), "seq", join_parts)
    top_score = jnp.maximum(cache_peak, new_peak)
    cache_factor = jnp.exp(cache_peak - top_score)
    new_factor = jnp.exp(new_peak - top_score)
    denominator = cache_total * cache_factor + new_total * new_factor
    attended = (
        cache_out * cache_factor[..., None] + new_out * new_factor[..., None]
    ) / denominator[..., None]
    attention = (
        attended.reshape(requests, kv_heads, drafts, group_size, head_dim)
        .transpose(0, 2, 1, 3, 4)
        .reshape(tokens, head_count * head_dim)
        .astype(jnp.bfloat16)
    )
    own_attention = lax.dynamic_slice_in_dim(attention, position * own_width, own_width, 1)
    own_output = lax.psum_scatter(
        lax.dot_general(
            out_weight, own_attention, (((0,), (1,)), ((), ())), preferred_element_type=jnp.float32
        ),
        "seq",
        scatter_dimension=0,
        tiled=True,
    )
    layer_output = own_output.T.reshape(requests, drafts, local_width).astype(jnp.bfloat16)
    return (layer_output, new_entries.reshape(requests, drafts, 2 * kv_heads * head_dim))


def step_kernel(
    kind_hbm, clen_hbm, slen_hbm, wlen_hbm, hidden_hbm, gain_hbm,
    qw_hbm, kvw_hbm, ow_hbm, rk_hbm, rv_hbm, sk_hbm, sv_hbm,
    out_ref, new_ref,
    kind_ref, clen_ref, slen_ref, wlen_ref, hidden_ref, gain_ref,
    w_buf, o_buf, rk, rv, sk, sv,
    sq_send, sq_recv, sib_send, sib_recv, rs_send, rs_recv, ag,
    a_res, stat_cols, a_send, a_recv, st_send, st_recv, o_send, o_recv,
    small_sem, load_sem, cache_sem, send_sem, recv_sem,
):
    f32, bf16 = jnp.float32, jnp.bfloat16
    n = lax.axis_size("seq")
    me = lax.axis_index("seq")
    core, chip, chips = lax.rem(me, 2), me // 2, n // 2
    sibling = me + 1 - 2 * core
    requests, drafts, width = hidden_ref.shape
    tokens = requests * drafts
    kv_heads = kind_ref.shape[0]
    retrieval, running = rk.shape[1], sk.shape[1]
    head_dim = rk.shape[3]
    own_width = o_buf.shape[1]
    piece = own_width + head_dim
    heads = own_width // head_dim
    share = n // kv_heads
    half_rows = heads * drafts
    own_rows = requests * half_rows
    group_rows = share * half_rows
    score_scale = head_dim ** (-0.5)
    exp_scale = score_scale * math.log2(math.e)
    SQ, SIB, RS, AG, STAT, OUT, ATT = range(7)

    def remote(kind, src, dst, send_slot, recv_slot, target):
        return pltpu.make_async_remote_copy(
            src_ref=src, dst_ref=dst,
            send_sem=send_sem.at[kind, send_slot], recv_sem=recv_sem.at[kind, recv_slot],
            device_id={"seq": target}, device_id_type=MESH,
        )

    def peer(step):
        return lax.rem(me + step, n)

    def each_peer(body):
        for step in range(1, n):
            body(step, peer(step))

    def arrived(buffer, sem):
        span = buffer.at[pl.ds(1, n - 1)]
        pltpu.make_async_copy(span, span, sem).wait()

    slabs = n // GROUP
    own_slab = me // GROUP

    def slab(k):
        return lax.rem(own_slab + 1 + k, slabs)

    def columns(k, size):
        return pl.ds(pl.multiple_of(slab(k) * (GROUP * size), GROUP * size), GROUP * size)

    def weight_copies(k):
        return (
            pltpu.make_async_copy(
                qw_hbm.at[:, columns(k, own_width)],
                w_buf.at[k, :, pl.ds(0, GROUP * own_width)], load_sem.at[0, k]),
            pltpu.make_async_copy(
                kvw_hbm.at[:, columns(k, head_dim)],
                w_buf.at[k, :, pl.ds(GROUP * own_width, GROUP * head_dim)], load_sem.at[1, k]),
        )

    def out_copy(k):
        return pltpu.make_async_copy(
            ow_hbm.at[:, columns(k, width)], o_buf.at[k], load_sem.at[2, k])

    small = [
        pltpu.make_async_copy(src, dst, small_sem.at[at]) for at, (src, dst) in enumerate((
            (hidden_hbm, hidden_ref), (gain_hbm, gain_ref), (kind_hbm, kind_ref),
            (clen_hbm, clen_ref), (slen_hbm, slen_ref), (wlen_hbm, wlen_ref)))
    ]
    for copy in small:
        copy.start()
    barrier = pltpu.get_barrier_semaphore()
    each_peer(lambda step, target: pl.semaphore_signal(
        barrier, inc=1, device_id={"seq": target}, device_id_type=MESH))
    for k in range(slabs):
        for copy in weight_copies(k):
            copy.start()

    for copy in small:
        copy.wait()
    hidden32 = jnp.concatenate([hidden_ref[b].astype(f32) for b in range(requests)], axis=0)
    squares = jnp.sum(hidden32 * hidden32, axis=-1, keepdims=True)
    eye = (lax.broadcasted_iota(jnp.int32, (tokens, 128), 0)
           == lax.broadcasted_iota(jnp.int32, (tokens, 128), 1))
    sq_send[...] = jnp.sum(jnp.where(eye, squares, 0.0), axis=0, keepdims=True)
    sq_recv[0] = sq_send[...]
    stat_cols[...] = jnp.zeros_like(stat_cols)
    pl.semaphore_wait(barrier, n - 1)

    def sq_copy(step, target):
        return remote(SQ, sq_send, sq_recv.at[step], 0, 0, target)

    each_peer(lambda step, target: sq_copy(step, target).start())

    cache_copies = [
        (pltpu.make_async_copy(sk_hbm, sk, cache_sem.at[0, 0]),
         pltpu.make_async_copy(sv_hbm, sv, cache_sem.at[1, 0])),
    ]
    for b in range(requests):
        cache_copies.append(
            (pltpu.make_async_copy(rk_hbm.at[b], rk.at[b], cache_sem.at[0, 1 + b]),
             pltpu.make_async_copy(rv_hbm.at[b], rv.at[b], cache_sem.at[1, 1 + b])))
    for pair in cache_copies:
        for copy in pair:
            copy.start()

    arrived(sq_recv, recv_sem.at[SQ, 0])
    total_row = sq_recv[0]
    for s in range(1, n):
        total_row = total_row + sq_recv[s]
    total_sq = jnp.sum(jnp.where(eye, total_row, 0.0), axis=1, keepdims=True)
    inverse = lax.rsqrt(total_sq / (width * n) + epsilon)
    normed = (hidden32 * inverse * gain_ref[...].astype(f32).reshape(1, width)).astype(bf16)

    def part(whole, owner):
        return jnp.concatenate(
            [whole[:, owner * own_width:(owner + 1) * own_width],
             whole[:, GROUP * own_width + owner * head_dim:
                   GROUP * own_width + (owner + 1) * head_dim]], axis=1)

    def pick(flag, first, second):
        return jnp.where(flag == 0, first, second)

    def sib_copy(k):
        return remote(SIB, sib_send.at[k], sib_recv.at[k], k, k, sibling)

    pairs = GROUP // 2
    own_pair = lax.rem(chip, pairs)

    def rs_copy(k, u):
        target = 2 * (slab(k) * pairs + u) + core
        return remote(
            RS, rs_send.at[k * pairs + u], rs_recv.at[k * pairs + own_pair],
            k * pairs + u, k * pairs + own_pair, target)

    def rs_arrival(k, u):
        return remote(
            RS, rs_send.at[0], rs_recv.at[k * pairs + u], 0, k * pairs + u, sibling)

    mine = []

    def send_sums(k):
        sib_copy(k).wait_recv()
        for u in range(pairs):
            rs_send[k * pairs + u] = mine[k][u] + sib_recv[k, u]
            rs_copy(k, u).start()

    for k in range(slabs):
        for copy in weight_copies(k):
            copy.wait()
        whole = jnp.dot(normed, w_buf[k], preferred_element_type=f32)
        sides = [(part(whole, 2 * u), part(whole, 2 * u + 1)) for u in range(pairs)]
        mine.append([pick(core, *side) for side in sides])
        for u in range(pairs):
            sib_send[k, u] = pick(core, sides[u][1], sides[u][0])
        sib_copy(k).start()
        if k > 0:
            send_sums(k - 1)

    last = slabs - 1
    sib_copy(last).wait_recv()
    for u in range(pairs):
        rs_send[last * pairs + u] = mine[last][u] + sib_recv[last, u]
    for hop in range(1, pairs):
        rs_copy(last, lax.rem(own_pair + hop, pairs)).start()
    own = rs_send[last * pairs + own_pair]

    for k in range(slabs):
        out_copy(k).start()

    for k in range(last):
        for u in range(pairs):
            rs_arrival(k, u).wait_recv()
            own = own + rs_recv[k * pairs + u]
    for hop in range(1, pairs):
        u = lax.rem(own_pair + hop, pairs)
        rs_arrival(last, u).wait_recv()
        own = own + rs_recv[last * pairs + u]

    def by_head(values):
        return jnp.concatenate(
            [values[b * drafts:(b + 1) * drafts, h * head_dim:(h + 1) * head_dim]
             for b in range(requests) for h in range(heads)], axis=0)

    packed = jnp.concatenate(
        [by_head(own[:, :own_width]), own[:, own_width:],
         jnp.zeros((ag.shape[2] - own_rows - tokens, head_dim), f32)], axis=0)
    ag[core, chip] = packed.astype(bf16)

    def ag_copy(step, target, source):
        return remote(
            AG, ag.at[core, source], ag.at[core, source], step, source, 2 * target + core)

    def each_chip(body):
        for step in range(1, chips):
            body(step, lax.rem(chip + step, chips))

    def pair_copy(side):
        return remote(AG, ag.at[side], ag.at[side], chips, chips, sibling)

    each_chip(lambda step, target: ag_copy(step, target, chip).start())

    kinds = [kind_ref[g] for g in range(kv_heads)]
    slot_of, before = [], 0
    for g in range(kv_heads):
        slot = jnp.where(kinds[g] == 1, before, retrieval + g - before)
        slot_of.append(jnp.minimum(slot, retrieval + running - 1))
        before = before + kinds[g]
    head_of = []
    for j in range(retrieval + running):
        found = 0
        for g in range(kv_heads):
            found = found + jnp.where(slot_of[g] == j, g, 0)
        head_of.append(jnp.minimum(found, kv_heads - 1))

    each_chip(lambda step, source: ag_copy(step, source, source).wait_recv())
    pair_copy(core).start()
    pair_copy(1 - core).wait_recv()

    for p in range(n):
        entries = ag[p % 2, p // 2, own_rows:, :]
        for b in range(requests):
            new_ref[b, :, p * head_dim:(p + 1) * head_dim] = entries[b * drafts:(b + 1) * drafts]

    def score(b, j, keys):
        q = jnp.concatenate(
            [ag[s % 2, head_of[j] * share // 2 + s // 2, b * half_rows:(b + 1) * half_rows, :]
             for s in range(share)], axis=0)
        return lax.dot_general(q, keys, (((1,), (1,)), ((), ())), preferred_element_type=f32)

    def attend(parts):
        scores = [jnp.where(seen, score(b, j, keys), floor_score)
                  for b, j, keys, _, seen in parts]
        peaks = [jnp.max(found, axis=-1, keepdims=True) for found in scores]
        weights = [jnp.exp2((found - peak) * exp_scale) for found, peak in zip(scores, peaks)]
        totals = [jnp.sum(weight, axis=-1, keepdims=True) for weight in weights]
        blocks = [jnp.dot(weight.astype(bf16), part[3], preferred_element_type=f32)
                  for weight, part in zip(weights, parts)]
        for part, block in zip(parts, blocks):
            b, j = part[0], part[1]
            a_res[j, :, b * half_rows:(b + 1) * half_rows, :] = block.astype(bf16).reshape(
                share, half_rows, head_dim)
        lane = lax.broadcasted_iota(jnp.int32, (half_rows, 128), 1)
        for b in sorted({part[0] for part in parts}):
            for at, columns_of in ((0, peaks), (own_rows, totals)):
                rows = pl.ds(at + b * half_rows, half_rows)
                kept = stat_cols[rows, :]
                for part, column in zip(parts, columns_of):
                    if part[0] == b:
                        for s in range(share):
                            kept = jnp.where(lane == share * head_of[part[1]] + s,
                                             column[s * half_rows:(s + 1) * half_rows], kept)
                stat_cols[rows, :] = kept

    for copy in cache_copies[0]:
        copy.wait()
    slots = sk.shape[2]
    slot_pos = me * slots + lax.broadcasted_iota(jnp.int32, (1, slots), 1)
    positions = rk.shape[2]
    cache_pos = me * positions + lax.broadcasted_iota(jnp.int32, (1, positions), 1)
    small_parts = []
    for b in range(requests):
        seen = (slot_pos < slen_ref[b]) | (
            (slot_pos >= SINK_CAP) & (slot_pos < SINK_CAP + wlen_ref[b]))
        for r in range(running):
            small_parts.append((b, retrieval + r, sk[b, r], sv[b, r], seen))
    attend(small_parts)

    def att_copy(b, step, target):
        rows = pl.ds(b * half_rows, half_rows)
        return remote(ATT + b, a_send.at[target, rows], a_recv.at[step, rows], 0, 0, target)

    for b in range(requests):
        for copy in cache_copies[1 + b]:
            copy.wait()
        seen = cache_pos < clen_ref[b]
        attend([(b, r, rk[b, r], rv[b, r], seen) for r in range(retrieval)])
        rows = slice(b * half_rows, (b + 1) * half_rows)
        for g in range(kv_heads):
            a_send[g * share:(g + 1) * share, rows] = a_res[slot_of[g], :, rows]
        a_recv[0, rows] = a_send[me, rows]
        if b < requests - 1:
            each_peer(lambda step, target: att_copy(b, step, target).start())

    lane = lax.broadcasted_iota(jnp.int32, (128, 128), 0)
    stat_rows = jnp.where(lane < own_rows, stat_cols[...] * score_scale, stat_cols[...]).T
    for p in range(n):
        st_send[p] = stat_rows[p:p + 1, :]
    st_recv[0] = st_send[me]

    def st_copy(step, target):
        return remote(STAT, st_send.at[target], st_recv.at[step], 0, 0, target)

    each_peer(lambda step, target: st_copy(step, target).start())
    each_peer(lambda step, target: att_copy(requests - 1, step, target).start())

    own_head = me // share
    own_q = ag[core, chip, 0:own_rows, :]
    new_keys = ag[lax.rem(own_head, 2), own_head // 2, own_rows:, :]
    new_values = ag[lax.rem(kv_heads + own_head, 2), (kv_heads + own_head) // 2, own_rows:, :]
    new_rows = ag.shape[2] - own_rows
    scores = lax.dot_general(own_q, new_keys, (((1,), (1,)), ((), ())), preferred_element_type=f32)
    scores = scores * score_scale
    row = lax.broadcasted_iota(jnp.int32, (own_rows, new_rows), 0)
    col = lax.broadcasted_iota(jnp.int32, (own_rows, new_rows), 1)
    row_bits, col_bits = half_rows.bit_length() - 1, drafts.bit_length() - 1
    same = lax.shift_right_logical(row, row_bits) == lax.shift_right_logical(col, col_bits)
    visible = same & ((col & (drafts - 1)) <= (row & (drafts - 1)))
    scores = jnp.where(visible, scores, floor_score)
    new_peak = jnp.max(scores, axis=-1, keepdims=True)
    new_weights = jnp.where(visible, jnp.exp(scores - new_peak), 0.0)
    new_total = jnp.sum(new_weights, axis=-1, keepdims=True)
    new_out = jnp.dot(new_weights.astype(bf16), new_values, preferred_element_type=f32)

    arrived(st_recv, recv_sem.at[STAT, 0])
    stats = jnp.concatenate(
        [st_recv[s] for s in range(n)] + [jnp.zeros((128 - n, 128), f32)], axis=0).T
    lane = lax.broadcasted_iota(jnp.int32, (own_rows, 128), 1)
    peaks = jnp.where(lane < n, stats[0:own_rows], floor_score)
    totals = stats[own_rows:2 * own_rows]
    top = jnp.maximum(jnp.max(peaks, axis=-1, keepdims=True), new_peak)
    factors = jnp.exp(peaks - top)
    new_factor = jnp.exp(new_peak - top)
    denominator = jnp.sum(factors * totals, axis=-1, keepdims=True) + new_factor * new_total
    numerator = new_factor * new_out
    for b in range(requests):
        arrived(a_recv.at[:, pl.ds(b * half_rows, half_rows)], recv_sem.at[ATT + b, 0])
    for s in range(n):
        numerator = numerator + factors[:, s:s + 1] * a_recv[s].astype(f32)
    attended = numerator / denominator
    attention = jnp.concatenate(
        [jnp.concatenate(
            [attended[b * half_rows + h * drafts:b * half_rows + (h + 1) * drafts]
             for b in range(requests)], axis=0) for h in range(heads)], axis=1).astype(bf16)

    half_width = width // 2

    def o_copy(k, at):
        owner = slab(k) * GROUP + at
        slot = k * GROUP + lax.rem(me, GROUP)
        return remote(OUT, o_send.at[k * GROUP + at], o_recv.at[slot], k * GROUP + at, slot, owner)

    def o_arrival(k, at):
        slot = k * GROUP + at
        return remote(OUT, o_send.at[0], o_recv.at[slot], 0, slot, sibling)

    own_at = lax.rem(me, GROUP)
    for k in range(slabs):
        out_copy(k).wait()
        whole = jnp.dot(attention, o_buf[k], preferred_element_type=f32)
        for at in range(GROUP):
            begin = at * width
            o_send[k * GROUP + at] = jnp.concatenate(
                [whole[:, begin:begin + half_width], whole[:, begin + half_width:begin + width]],
                axis=0).astype(bf16)
            if k < slabs - 1:
                o_copy(k, at).start()
    for hop in range(1, GROUP):
        o_copy(slabs - 1, lax.rem(own_at + hop, GROUP)).start()
    result = o_send[(slabs - 1) * GROUP + own_at].astype(f32)
    for k in range(slabs):
        for at in range(GROUP):
            if k < slabs - 1:
                o_arrival(k, at).wait_recv()
                result = result + o_recv[k * GROUP + at].astype(f32)
            elif at > 0:
                place = lax.rem(own_at + at, GROUP)
                o_arrival(k, place).wait_recv()
                result = result + o_recv[k * GROUP + place].astype(f32)
    result = jnp.concatenate([result[:tokens], result[tokens:]], axis=1).astype(bf16)
    for b in range(requests):
        out_ref[b] = result[b * drafts:(b + 1) * drafts]

    arrived(sq_recv, send_sem.at[SQ, 0])
    arrived(st_recv, send_sem.at[STAT, 0])
    for b in range(requests):
        arrived(a_recv.at[:, pl.ds(b * half_rows, half_rows)], send_sem.at[ATT + b, 0])
    each_chip(lambda step, target: ag_copy(step, target, chip).wait_send())
    pair_copy(core).wait_send()
    for k in range(slabs):
        sib_copy(k).wait_send()
        if k < last:
            for u in range(pairs):
                rs_copy(k, u).wait_send()
            for at in range(GROUP):
                o_copy(k, at).wait_send()
    for hop in range(1, pairs):
        rs_copy(last, lax.rem(own_pair + hop, pairs)).wait_send()
    for hop in range(1, GROUP):
        o_copy(last, lax.rem(own_at + hop, GROUP)).wait_send()


def fused_device(
    hidden, norm_gain, q_weight, kv_weight, out_weight, head_kind,
    ret_keys, ret_values, stream_keys, stream_values, cache_len, sink_len, window_len,
):
    n = lax.axis_size("seq")
    requests, drafts, width = hidden.shape
    tokens = requests * drafts
    head_dim = ret_keys.shape[3]
    own_width = out_weight.shape[0]
    own_rows = tokens * (own_width // head_dim)
    slots = ret_keys.shape[1] + stream_keys.shape[1]
    share = n // slots
    chips = n // 2
    piece = own_width + head_dim
    f32, bf16 = jnp.float32, jnp.bfloat16
    vmem = pl.BlockSpec(memory_space=pltpu.VMEM)
    hbm = pl.BlockSpec(memory_space=pltpu.HBM)
    scratch = [
        pltpu.SMEM(head_kind.shape, jnp.int32),
        pltpu.SMEM(cache_len.shape, jnp.int32),
        pltpu.SMEM(sink_len.shape, jnp.int32),
        pltpu.SMEM(window_len.shape, jnp.int32),
        pltpu.VMEM(hidden.shape, bf16),
        pltpu.VMEM(norm_gain.shape, bf16),
        pltpu.VMEM((n // GROUP, width, GROUP * piece), bf16),
        pltpu.VMEM((n // GROUP, own_width, GROUP * width), bf16),
        pltpu.VMEM(ret_keys.shape, bf16),
        pltpu.VMEM(ret_values.shape, bf16),
        pltpu.VMEM(stream_keys.shape, bf16),
        pltpu.VMEM(stream_values.shape, bf16),
        pltpu.VMEM((1, 128), f32),
        pltpu.VMEM((n, 1, 128), f32),
        pltpu.VMEM((n // GROUP, GROUP // 2, tokens, piece), f32),
        pltpu.VMEM((n // GROUP, GROUP // 2, tokens, piece), f32),
        pltpu.VMEM((chips, tokens, piece), f32),
        pltpu.VMEM((chips, tokens, piece), f32),
        pltpu.VMEM((2, chips, own_rows + 16, head_dim), bf16),
        pltpu.VMEM((slots, share, own_rows, head_dim), bf16),
        pltpu.VMEM((128, 128), f32),
        pltpu.VMEM((n, own_rows, head_dim), bf16),
        pltpu.VMEM((n, own_rows, head_dim), bf16),
        pltpu.VMEM((n, 1, 128), f32),
        pltpu.VMEM((n, 1, 128), f32),
        pltpu.VMEM((n, 2 * tokens, width // 2), bf16),
        pltpu.VMEM((n, 2 * tokens, width // 2), bf16),
        pltpu.SemaphoreType.DMA((6,)),
        pltpu.SemaphoreType.DMA((3, n)),
        pltpu.SemaphoreType.DMA((2, 1 + requests)),
        pltpu.SemaphoreType.DMA((6 + requests, n)),
        pltpu.SemaphoreType.DMA((6 + requests, n)),
    ]
    return pl.pallas_call(
        step_kernel,
        out_shape=(
            pltpu.VMEM(hidden.shape, bf16),
            pltpu.VMEM((requests, drafts, kv_weight.shape[1]), bf16),
        ),
        in_specs=[hbm] * 13,
        out_specs=(vmem, vmem),
        scratch_shapes=scratch,
        compiler_params=pltpu.CompilerParams(
            collective_id=0, has_side_effects=True, vmem_limit_bytes=62 * 2**20
        ),
        name="decode_step",
    )(
        head_kind, cache_len, sink_len, window_len, hidden, norm_gain,
        q_weight, kv_weight, out_weight, ret_keys, ret_values, stream_keys, stream_values,
    )


def power_of_two(value):
    return value & (value - 1) == 0


def fused_fits(
    hidden, norm_gain, q_weight, kv_weight, out_weight, head_kind,
    ret_keys, ret_values, stream_keys, stream_values, cache_len, sink_len, window_len,
):
    n = lax.axis_size("seq")
    requests, drafts, width = hidden.shape
    tokens = requests * drafts
    head_dim = ret_keys.shape[3]
    own_width = out_weight.shape[0]
    kv_heads = head_kind.shape[0]
    heads = own_width // head_dim
    return (
        n % (2 * GROUP) == 0 and n <= 128 and n % kv_heads == 0 and tokens == 8
        and head_dim == 128 and width % 256 == 0 and own_width % head_dim == 0
        and q_weight.shape[1] == n * own_width and kv_weight.shape[1] == n * head_dim
        and n == 2 * kv_heads and power_of_two(heads * drafts) and power_of_two(drafts)
        and heads * drafts % 16 == 0 and 2 * tokens * heads <= 128
        and ret_keys.shape[2] % 128 == 0 and stream_keys.shape[2] % 128 == 0
        and ret_keys.shape[1] + stream_keys.shape[1] == kv_heads
    )


def step_device(*args):
    return fused_device(*args) if fused_fits(*args) else per_device(*args)


def solution(mesh):
    in_specs = (
        P("groups", None, "seq"),
        P("seq"),
        P("seq", None),
        P("seq", None),
        P("seq", None),
        P(),
        P("groups", None, "seq", None),
        P("groups", None, "seq", None),
        P("groups", None, "seq", None),
        P("groups", None, "seq", None),
        P("groups"),
        P("groups"),
        P("groups"),
    )
    out_specs = (P("groups", None, "seq"), P("groups", None, None))
    return jax.shard_map(
        step_device, mesh=mesh, in_specs=in_specs, out_specs=out_specs, check_vma=False
    )
```

```python
import math

import jax
import jax.numpy as jnp
from jax import lax
from jax.experimental import pallas as pl
from jax.experimental.pallas import tpu as pltpu
from jax.sharding import PartitionSpec as P

SINK_CAP = 128
MESH = pl.DeviceIdType.MESH
GROUP = 4


epsilon = 1e-05
floor_score = -1e30


def joined(part, axis, combine):
    gathered = jax.tree.map(lambda a: lax.all_gather(a, axis), part)

    def take(source):
        return jax.tree.map(lambda a: lax.dynamic_index_in_dim(a, source, 0, False), gathered)

    return lax.fori_loop(
        1, lax.axis_size(axis), lambda source, state: combine(state, take(source)), take(0)
    )


def block_stats(queries, cache_keys, cache_values, visible, score_scale):
    scores = (
        jnp.einsum("bhqd,bhld->bhql", queries, cache_keys, preferred_element_type=jnp.float32)
        * score_scale
    )
    scores = jnp.where(visible, scores, floor_score)
    peak_score = jnp.max(scores, axis=-1)
    weights = jnp.where(visible, jnp.exp(scores - peak_score[..., None]), 0.0)
    weight_total = jnp.sum(weights, axis=-1)
    block_out = jnp.einsum(
        "bhql,bhld->bhqd",
        weights.astype(jnp.bfloat16),
        cache_values,
        preferred_element_type=jnp.float32,
    )
    return (peak_score, weight_total, block_out)


def spread_rows(values_in, selector):
    return jnp.einsum("brq,gr->bgq", values_in, selector, precision=lax.Precision.HIGHEST)


def spread_vectors(values_in, selector):
    return jnp.einsum("brqd,gr->bgqd", values_in, selector, precision=lax.Precision.HIGHEST)


def join_parts(first_part, second_part):
    top_score = jnp.maximum(first_part[0], second_part[0])
    left_factor = jnp.exp(first_part[0] - top_score)
    right_factor = jnp.exp(second_part[0] - top_score)
    joined_total = first_part[1] * left_factor + second_part[1] * right_factor
    joined_out = first_part[2] * left_factor[..., None] + second_part[2] * right_factor[..., None]
    return (top_score, joined_total, joined_out)


def per_device(
    hidden,
    norm_gain,
    q_weight,
    kv_weight,
    out_weight,
    head_kind,
    ret_keys,
    ret_values,
    stream_keys,
    stream_values,
    cache_len,
    sink_len,
    window_len,
):
    requests, drafts, local_width = hidden.shape
    kv_heads = head_kind.shape[0]
    head_dim = ret_keys.shape[3]
    retrieval = ret_keys.shape[1]
    running = stream_keys.shape[1]
    head_count = q_weight.shape[1] // head_dim
    group_size = head_count // kv_heads
    query_rows = drafts * group_size
    devices = lax.axis_size("seq")
    position = lax.axis_index("seq")
    tokens = requests * drafts
    hidden32 = hidden.astype(jnp.float32)
    squares = lax.psum(jnp.sum(hidden32 * hidden32, axis=-1), "seq")
    inverse = lax.rsqrt(squares / (local_width * devices) + epsilon)
    normed = (hidden32 * inverse[..., None] * norm_gain.astype(jnp.float32)).astype(jnp.bfloat16)
    flat_rows = normed.reshape(tokens, local_width)
    part_query = jnp.dot(flat_rows, q_weight, preferred_element_type=jnp.float32)
    part_fresh = jnp.dot(flat_rows, kv_weight, preferred_element_type=jnp.float32)
    whole_query, whole_fresh = lax.psum((part_query, part_fresh), "seq")
    queries = whole_query.astype(jnp.bfloat16)
    new_entries = whole_fresh.astype(jnp.bfloat16)
    grouped = (
        queries.reshape(requests, drafts, kv_heads, group_size, head_dim)
        .transpose(0, 2, 1, 3, 4)
        .reshape(requests, kv_heads, query_rows, head_dim)
    )
    fresh_split = new_entries.reshape(requests, drafts, 2, kv_heads, head_dim)
    new_keys = fresh_split[:, :, 0].transpose(0, 2, 1, 3)
    new_values = fresh_split[:, :, 1].transpose(0, 2, 1, 3)
    kind_flag = head_kind == 1
    rank_ret = jnp.cumsum(head_kind) - 1
    rank_str = jnp.cumsum(1 - head_kind) - 1
    select_ret = (
        kind_flag[:, None] & (rank_ret[:, None] == jnp.arange(retrieval)[None, :])
    ).astype(jnp.float32)
    select_str = (
        jnp.logical_not(kind_flag)[:, None] & (rank_str[:, None] == jnp.arange(running)[None, :])
    ).astype(jnp.float32)
    ret_queries = jnp.einsum(
        "bgqd,gr->brqd",
        grouped,
        select_ret.astype(jnp.bfloat16),
        preferred_element_type=jnp.float32,
    ).astype(jnp.bfloat16)
    str_queries = jnp.einsum(
        "bgqd,gr->brqd",
        grouped,
        select_str.astype(jnp.bfloat16),
        preferred_element_type=jnp.float32,
    ).astype(jnp.bfloat16)
    score_scale = head_dim ** (-0.5)
    cache_block = ret_keys.shape[2]
    cache_pos = position * cache_block + jnp.arange(cache_block)
    ret_visible = (cache_pos[None, :] < cache_len[:, None])[:, None, None, :]
    slot_block = stream_keys.shape[2]
    slot_pos = (position * slot_block + jnp.arange(slot_block))[None, :]
    sink_part = slot_pos < sink_len[:, None]
    recent_part = (slot_pos >= SINK_CAP) & (slot_pos < SINK_CAP + window_len[:, None])
    str_visible = (sink_part | recent_part)[:, None, None, :]
    ret_peak, ret_total, ret_out = block_stats(
        ret_queries, ret_keys, ret_values, ret_visible, score_scale
    )
    str_peak, str_total, str_out = block_stats(
        str_queries, stream_keys, stream_values, str_visible, score_scale
    )
    peak_all = spread_rows(ret_peak, select_ret) + spread_rows(str_peak, select_str)
    total_all = spread_rows(ret_total, select_ret) + spread_rows(str_total, select_str)
    out_all = spread_vectors(ret_out, select_ret) + spread_vectors(str_out, select_str)
    token_of_row = jnp.arange(query_rows) // group_size
    new_visible = jnp.arange(drafts)[None, :] <= token_of_row[:, None]
    new_peak, new_total, new_out = block_stats(
        grouped, new_keys, new_values, new_visible, score_scale
    )
    own_width = out_weight.shape[0]
    cache_peak, cache_total, cache_out = joined((peak_all, total_all, out_all), "seq", join_parts)
    top_score = jnp.maximum(cache_peak, new_peak)
    cache_factor = jnp.exp(cache_peak - top_score)
    new_factor = jnp.exp(new_peak - top_score)
    denominator = cache_total * cache_factor + new_total * new_factor
    attended = (
        cache_out * cache_factor[..., None] + new_out * new_factor[..., None]
    ) / denominator[..., None]
    attention = (
        attended.reshape(requests, kv_heads, drafts, group_size, head_dim)
        .transpose(0, 2, 1, 3, 4)
        .reshape(tokens, head_count * head_dim)
        .astype(jnp.bfloat16)
    )
    own_attention = lax.dynamic_slice_in_dim(attention, position * own_width, own_width, 1)
    own_output = lax.psum_scatter(
        lax.dot_general(
            out_weight, own_attention, (((0,), (1,)), ((), ())), preferred_element_type=jnp.float32
        ),
        "seq",
        scatter_dimension=0,
        tiled=True,
    )
    layer_output = own_output.T.reshape(requests, drafts, local_width).astype(jnp.bfloat16)
    return (layer_output, new_entries.reshape(requests, drafts, 2 * kv_heads * head_dim))


def step_kernel(
    kind_hbm, clen_hbm, slen_hbm, wlen_hbm, hidden_hbm, gain_hbm,
    qw_hbm, kvw_hbm, ow_hbm, rk_hbm, rv_hbm, sk_hbm, sv_hbm,
    out_ref, new_ref,
    kind_ref, clen_ref, slen_ref, wlen_ref, hidden_ref, gain_ref,
    w_buf, o_buf, rk, rv, sk, sv,
    sq_send, sq_recv, sib_send, sib_recv, quad_send, quad_recv, rs_send, rs_recv, ag,
    a_res, stat_cols, a_send, a_recv, st_send, st_recv, o_send, o_recv,
    small_sem, load_sem, cache_sem, send_sem, recv_sem,
):
    f32, bf16 = jnp.float32, jnp.bfloat16
    n = lax.axis_size("seq")
    me = lax.axis_index("seq")
    core, chip, chips = lax.rem(me, 2), me // 2, n // 2
    sibling = me + 1 - 2 * core
    requests, drafts, width = hidden_ref.shape
    tokens = requests * drafts
    kv_heads = kind_ref.shape[0]
    retrieval, running = rk.shape[1], sk.shape[1]
    head_dim = rk.shape[3]
    own_width = o_buf.shape[1]
    piece = own_width + head_dim
    heads = own_width // head_dim
    share = n // kv_heads
    half_rows = heads * drafts
    own_rows = requests * half_rows
    group_rows = share * half_rows
    score_scale = head_dim ** (-0.5)
    exp_scale = score_scale * math.log2(math.e)
    SQ, SIB, RS, AG, STAT, OUT, QUAD, ATT = range(8)

    def remote(kind, src, dst, send_slot, recv_slot, target):
        return pltpu.make_async_remote_copy(
            src_ref=src, dst_ref=dst,
            send_sem=send_sem.at[kind, send_slot], recv_sem=recv_sem.at[kind, recv_slot],
            device_id={"seq": target}, device_id_type=MESH,
        )

    def peer(step):
        return lax.rem(me + step, n)

    def each_peer(body):
        for step in range(1, n):
            body(step, peer(step))

    def arrived(buffer, sem):
        span = buffer.at[pl.ds(1, n - 1)]
        pltpu.make_async_copy(span, span, sem).wait()

    slabs = n // GROUP
    own_slab = me // GROUP

    def slab(k):
        return lax.rem(own_slab + 1 + k, slabs)

    def columns(k, size):
        return pl.ds(pl.multiple_of(slab(k) * (GROUP * size), GROUP * size), GROUP * size)

    def weight_copies(k):
        return (
            pltpu.make_async_copy(
                qw_hbm.at[:, columns(k, own_width)],
                w_buf.at[k, :, pl.ds(0, GROUP * own_width)], load_sem.at[0, k]),
            pltpu.make_async_copy(
                kvw_hbm.at[:, columns(k, head_dim)],
                w_buf.at[k, :, pl.ds(GROUP * own_width, GROUP * head_dim)], load_sem.at[1, k]),
        )

    def out_copy(k):
        return pltpu.make_async_copy(
            ow_hbm.at[:, columns(k, width)], o_buf.at[k], load_sem.at[2, k])

    small = [
        pltpu.make_async_copy(src, dst, small_sem.at[at]) for at, (src, dst) in enumerate((
            (hidden_hbm, hidden_ref), (gain_hbm, gain_ref), (kind_hbm, kind_ref),
            (clen_hbm, clen_ref), (slen_hbm, slen_ref), (wlen_hbm, wlen_ref)))
    ]
    for copy in small:
        copy.start()
    barrier = pltpu.get_barrier_semaphore()
    each_peer(lambda step, target: pl.semaphore_signal(
        barrier, inc=1, device_id={"seq": target}, device_id_type=MESH))
    for k in range(slabs):
        for copy in weight_copies(k):
            copy.start()

    for copy in small:
        copy.wait()
    hidden32 = jnp.concatenate([hidden_ref[b].astype(f32) for b in range(requests)], axis=0)
    squares = jnp.sum(hidden32 * hidden32, axis=-1, keepdims=True)
    eye = (lax.broadcasted_iota(jnp.int32, (tokens, 128), 0)
           == lax.broadcasted_iota(jnp.int32, (tokens, 128), 1))
    sq_send[...] = jnp.sum(jnp.where(eye, squares, 0.0), axis=0, keepdims=True)
    sq_recv[0] = sq_send[...]
    stat_cols[...] = jnp.zeros_like(stat_cols)
    pl.semaphore_wait(barrier, n - 1)

    def sq_copy(step, target):
        return remote(SQ, sq_send, sq_recv.at[step], 0, 0, target)

    each_peer(lambda step, target: sq_copy(step, target).start())

    cache_copies = [
        (pltpu.make_async_copy(sk_hbm, sk, cache_sem.at[0, 0]),
         pltpu.make_async_copy(sv_hbm, sv, cache_sem.at[1, 0])),
    ]
    for b in range(requests):
        cache_copies.append(
            (pltpu.make_async_copy(rk_hbm.at[b], rk.at[b], cache_sem.at[0, 1 + b]),
             pltpu.make_async_copy(rv_hbm.at[b], rv.at[b], cache_sem.at[1, 1 + b])))
    arrived(sq_recv, recv_sem.at[SQ, 0])
    total_row = sq_recv[0]
    for s in range(1, n):
        total_row = total_row + sq_recv[s]
    total_sq = jnp.sum(jnp.where(eye, total_row, 0.0), axis=1, keepdims=True)
    inverse = lax.rsqrt(total_sq / (width * n) + epsilon)
    normed = (hidden32 * inverse * gain_ref[...].astype(f32).reshape(1, width)).astype(bf16)

    def part(whole, owner):
        return jnp.concatenate(
            [whole[:, owner * own_width:(owner + 1) * own_width],
             whole[:, GROUP * own_width + owner * head_dim:
                   GROUP * own_width + (owner + 1) * head_dim]], axis=1)

    def pick(flag, first, second):
        return jnp.where(flag == 0, first, second)

    def sib_copy(k):
        return remote(SIB, sib_send.at[k], sib_recv.at[k], k, k, sibling)

    pairs = GROUP // 2
    own_pair = lax.rem(chip, pairs)

    def rs_copy(k, u):
        target = 2 * (slab(k) * pairs + u) + core
        return remote(
            RS, rs_send.at[k * pairs + u], rs_recv.at[k * pairs + own_pair],
            k * pairs + u, k * pairs + own_pair, target)

    def rs_arrival(k, u):
        return remote(
            RS, rs_send.at[0], rs_recv.at[k * pairs + u], 0, k * pairs + u, sibling)

    own_at = lax.rem(me, GROUP)
    last = slabs - 1
    others = [lax.rem(own_at + hop, GROUP) for hop in range(1, GROUP)]

    def quad_copy(at):
        return remote(
            QUAD, quad_send.at[at], quad_recv.at[own_at], at, own_at, own_slab * GROUP + at)

    def quad_arrival(at):
        return remote(QUAD, quad_send.at[0], quad_recv.at[at], 0, at, sibling)

    mine = []

    def send_sums(k):
        sib_copy(k).wait_recv()
        for u in range(pairs):
            rs_send[k * pairs + u] = mine[k][u] + sib_recv[k, u]
            rs_copy(k, u).start()

    for k in range(slabs):
        for copy in weight_copies(k):
            copy.wait()
        whole = jnp.dot(normed, w_buf[k], preferred_element_type=f32)
        if k == 1:
            for pair in cache_copies:
                for copy in pair:
                    copy.start()
        if k < last:
            sides = [(part(whole, 2 * u), part(whole, 2 * u + 1)) for u in range(pairs)]
            mine.append([pick(core, *side) for side in sides])
            for u in range(pairs):
                sib_send[k, u] = pick(core, sides[u][1], sides[u][0])
            sib_copy(k).start()
        else:
            for at in range(GROUP):
                quad_send[at] = part(whole, at)
            for at in others:
                quad_copy(at).start()
        if k > 0:
            send_sums(k - 1)

    own = quad_send[own_at]

    for k in range(slabs):
        out_copy(k).start()

    for k in range(last):
        for u in range(pairs):
            rs_arrival(k, u).wait_recv()
            own = own + rs_recv[k * pairs + u]
    for at in others:
        quad_arrival(at).wait_recv()
        own = own + quad_recv[at]

    def by_head(values):
        return jnp.concatenate(
            [values[b * drafts:(b + 1) * drafts, h * head_dim:(h + 1) * head_dim]
             for b in range(requests) for h in range(heads)], axis=0)

    packed = jnp.concatenate(
        [by_head(own[:, :own_width]), own[:, own_width:],
         jnp.zeros((ag.shape[2] - own_rows - tokens, head_dim), f32)], axis=0)
    ag[core, chip] = packed.astype(bf16)

    def ag_copy(step, target, source):
        return remote(
            AG, ag.at[core, source], ag.at[core, source], step, source, 2 * target + core)

    def each_chip(body):
        for step in range(1, chips):
            body(step, lax.rem(chip + step, chips))

    def pair_copy(side):
        return remote(AG, ag.at[side], ag.at[side], chips, chips, sibling)

    each_chip(lambda step, target: ag_copy(step, target, chip).start())

    kinds = [kind_ref[g] for g in range(kv_heads)]
    slot_of, before = [], 0
    for g in range(kv_heads):
        slot = jnp.where(kinds[g] == 1, before, retrieval + g - before)
        slot_of.append(jnp.minimum(slot, retrieval + running - 1))
        before = before + kinds[g]
    head_of = []
    for j in range(retrieval + running):
        found = 0
        for g in range(kv_heads):
            found = found + jnp.where(slot_of[g] == j, g, 0)
        head_of.append(jnp.minimum(found, kv_heads - 1))

    each_chip(lambda step, source: ag_copy(step, source, source).wait_recv())
    pair_copy(core).start()
    pair_copy(1 - core).wait_recv()

    for p in range(n):
        entries = ag[p % 2, p // 2, own_rows:, :]
        for b in range(requests):
            new_ref[b, :, p * head_dim:(p + 1) * head_dim] = entries[b * drafts:(b + 1) * drafts]

    def score(b, j, keys):
        q = jnp.concatenate(
            [ag[s % 2, head_of[j] * share // 2 + s // 2, b * half_rows:(b + 1) * half_rows, :]
             for s in range(share)], axis=0)
        return lax.dot_general(q, keys, (((1,), (1,)), ((), ())), preferred_element_type=f32)

    def attend(parts):
        scores = [jnp.where(seen, score(b, j, keys), floor_score)
                  for b, j, keys, _, seen in parts]
        peaks = [jnp.max(found, axis=-1, keepdims=True) for found in scores]
        weights = [jnp.exp2((found - peak) * exp_scale) for found, peak in zip(scores, peaks)]
        totals = [jnp.sum(weight, axis=-1, keepdims=True) for weight in weights]
        blocks = [jnp.dot(weight.astype(bf16), part[3], preferred_element_type=f32)
                  for weight, part in zip(weights, parts)]
        for part, block in zip(parts, blocks):
            b, j = part[0], part[1]
            a_res[j, :, b * half_rows:(b + 1) * half_rows, :] = block.astype(bf16).reshape(
                share, half_rows, head_dim)
        lane = lax.broadcasted_iota(jnp.int32, (half_rows, 128), 1)
        for b in sorted({part[0] for part in parts}):
            for at, columns_of in ((0, peaks), (own_rows, totals)):
                rows = pl.ds(at + b * half_rows, half_rows)
                kept = stat_cols[rows, :]
                for part, column in zip(parts, columns_of):
                    if part[0] == b:
                        for s in range(share):
                            kept = jnp.where(lane == share * head_of[part[1]] + s,
                                             column[s * half_rows:(s + 1) * half_rows], kept)
                stat_cols[rows, :] = kept

    for copy in cache_copies[0]:
        copy.wait()
    slots = sk.shape[2]
    slot_pos = me * slots + lax.broadcasted_iota(jnp.int32, (1, slots), 1)
    positions = rk.shape[2]
    cache_pos = me * positions + lax.broadcasted_iota(jnp.int32, (1, positions), 1)
    small_parts = []
    for b in range(requests):
        seen = (slot_pos < slen_ref[b]) | (
            (slot_pos >= SINK_CAP) & (slot_pos < SINK_CAP + wlen_ref[b]))
        for r in range(running):
            small_parts.append((b, retrieval + r, sk[b, r], sv[b, r], seen))
    attend(small_parts)

    def att_copy(b, step, target):
        rows = pl.ds(b * half_rows, half_rows)
        return remote(ATT + b, a_send.at[target, rows], a_recv.at[step, rows], 0, 0, target)

    for b in range(requests):
        for copy in cache_copies[1 + b]:
            copy.wait()
        seen = cache_pos < clen_ref[b]
        attend([(b, r, rk[b, r], rv[b, r], seen) for r in range(retrieval)])
        rows = slice(b * half_rows, (b + 1) * half_rows)
        for g in range(kv_heads):
            a_send[g * share:(g + 1) * share, rows] = a_res[slot_of[g], :, rows]
        a_recv[0, rows] = a_send[me, rows]
        if b < requests - 1:
            each_peer(lambda step, target: att_copy(b, step, target).start())

    lane = lax.broadcasted_iota(jnp.int32, (128, 128), 0)
    stat_rows = jnp.where(lane < own_rows, stat_cols[...] * score_scale, stat_cols[...]).T
    for p in range(n):
        st_send[p] = stat_rows[p:p + 1, :]
    st_recv[0] = st_send[me]

    def st_copy(step, target):
        return remote(STAT, st_send.at[target], st_recv.at[step], 0, 0, target)

    each_peer(lambda step, target: st_copy(step, target).start())
    each_peer(lambda step, target: att_copy(requests - 1, step, target).start())

    own_head = me // share
    own_q = ag[core, chip, 0:own_rows, :]
    new_keys = ag[lax.rem(own_head, 2), own_head // 2, own_rows:, :]
    new_values = ag[lax.rem(kv_heads + own_head, 2), (kv_heads + own_head) // 2, own_rows:, :]
    new_rows = ag.shape[2] - own_rows
    scores = lax.dot_general(own_q, new_keys, (((1,), (1,)), ((), ())), preferred_element_type=f32)
    scores = scores * score_scale
    row = lax.broadcasted_iota(jnp.int32, (own_rows, new_rows), 0)
    col = lax.broadcasted_iota(jnp.int32, (own_rows, new_rows), 1)
    row_bits, col_bits = half_rows.bit_length() - 1, drafts.bit_length() - 1
    same = lax.shift_right_logical(row, row_bits) == lax.shift_right_logical(col, col_bits)
    visible = same & ((col & (drafts - 1)) <= (row & (drafts - 1)))
    scores = jnp.where(visible, scores, floor_score)
    new_peak = jnp.max(scores, axis=-1, keepdims=True)
    new_weights = jnp.where(visible, jnp.exp(scores - new_peak), 0.0)
    new_total = jnp.sum(new_weights, axis=-1, keepdims=True)
    new_out = jnp.dot(new_weights.astype(bf16), new_values, preferred_element_type=f32)

    arrived(st_recv, recv_sem.at[STAT, 0])
    stats = jnp.concatenate(
        [st_recv[s] for s in range(n)] + [jnp.zeros((128 - n, 128), f32)], axis=0).T
    lane = lax.broadcasted_iota(jnp.int32, (own_rows, 128), 1)
    peaks = jnp.where(lane < n, stats[0:own_rows], floor_score)
    totals = stats[own_rows:2 * own_rows]
    top = jnp.maximum(jnp.max(peaks, axis=-1, keepdims=True), new_peak)
    factors = jnp.exp(peaks - top)
    new_factor = jnp.exp(new_peak - top)
    denominator = jnp.sum(factors * totals, axis=-1, keepdims=True) + new_factor * new_total
    numerator = new_factor * new_out
    for b in range(requests):
        arrived(a_recv.at[:, pl.ds(b * half_rows, half_rows)], recv_sem.at[ATT + b, 0])
    for s in range(n):
        numerator = numerator + factors[:, s:s + 1] * a_recv[s].astype(f32)
    attended = numerator / denominator
    attention = jnp.concatenate(
        [jnp.concatenate(
            [attended[b * half_rows + h * drafts:b * half_rows + (h + 1) * drafts]
             for b in range(requests)], axis=0) for h in range(heads)], axis=1).astype(bf16)

    half_width = width // 2

    def o_copy(k, at):
        owner = slab(k) * GROUP + at
        slot = k * GROUP + lax.rem(me, GROUP)
        return remote(OUT, o_send.at[k * GROUP + at], o_recv.at[slot], k * GROUP + at, slot, owner)

    def o_arrival(k, at):
        slot = k * GROUP + at
        return remote(OUT, o_send.at[0], o_recv.at[slot], 0, slot, sibling)

    for k in range(slabs):
        out_copy(k).wait()
        whole = jnp.dot(attention, o_buf[k], preferred_element_type=f32)
        for at in range(GROUP):
            begin = at * width
            o_send[k * GROUP + at] = jnp.concatenate(
                [whole[:, begin:begin + half_width], whole[:, begin + half_width:begin + width]],
                axis=0).astype(bf16)
            if k < slabs - 1:
                o_copy(k, at).start()
    for hop in range(1, GROUP):
        o_copy(slabs - 1, lax.rem(own_at + hop, GROUP)).start()
    result = o_send[(slabs - 1) * GROUP + own_at].astype(f32)
    for k in range(slabs):
        for at in range(GROUP):
            if k < slabs - 1:
                o_arrival(k, at).wait_recv()
                result = result + o_recv[k * GROUP + at].astype(f32)
            elif at > 0:
                place = lax.rem(own_at + at, GROUP)
                o_arrival(k, place).wait_recv()
                result = result + o_recv[k * GROUP + place].astype(f32)
    result = jnp.concatenate([result[:tokens], result[tokens:]], axis=1).astype(bf16)
    for b in range(requests):
        out_ref[b] = result[b * drafts:(b + 1) * drafts]

    arrived(sq_recv, send_sem.at[SQ, 0])
    arrived(st_recv, send_sem.at[STAT, 0])
    for b in range(requests):
        arrived(a_recv.at[:, pl.ds(b * half_rows, half_rows)], send_sem.at[ATT + b, 0])
    each_chip(lambda step, target: ag_copy(step, target, chip).wait_send())
    pair_copy(core).wait_send()
    for k in range(last):
        sib_copy(k).wait_send()
        for u in range(pairs):
            rs_copy(k, u).wait_send()
        for at in range(GROUP):
            o_copy(k, at).wait_send()
    for at in others:
        quad_copy(at).wait_send()
    for hop in range(1, GROUP):
        o_copy(last, lax.rem(own_at + hop, GROUP)).wait_send()


def fused_device(
    hidden, norm_gain, q_weight, kv_weight, out_weight, head_kind,
    ret_keys, ret_values, stream_keys, stream_values, cache_len, sink_len, window_len,
):
    n = lax.axis_size("seq")
    requests, drafts, width = hidden.shape
    tokens = requests * drafts
    head_dim = ret_keys.shape[3]
    own_width = out_weight.shape[0]
    own_rows = tokens * (own_width // head_dim)
    slots = ret_keys.shape[1] + stream_keys.shape[1]
    share = n // slots
    chips = n // 2
    piece = own_width + head_dim
    f32, bf16 = jnp.float32, jnp.bfloat16
    vmem = pl.BlockSpec(memory_space=pltpu.VMEM)
    hbm = pl.BlockSpec(memory_space=pltpu.HBM)
    scratch = [
        pltpu.SMEM(head_kind.shape, jnp.int32),
        pltpu.SMEM(cache_len.shape, jnp.int32),
        pltpu.SMEM(sink_len.shape, jnp.int32),
        pltpu.SMEM(window_len.shape, jnp.int32),
        pltpu.VMEM(hidden.shape, bf16),
        pltpu.VMEM(norm_gain.shape, bf16),
        pltpu.VMEM((n // GROUP, width, GROUP * piece), bf16),
        pltpu.VMEM((n // GROUP, own_width, GROUP * width), bf16),
        pltpu.VMEM(ret_keys.shape, bf16),
        pltpu.VMEM(ret_values.shape, bf16),
        pltpu.VMEM(stream_keys.shape, bf16),
        pltpu.VMEM(stream_values.shape, bf16),
        pltpu.VMEM((1, 128), f32),
        pltpu.VMEM((n, 1, 128), f32),
        pltpu.VMEM((n // GROUP - 1, GROUP // 2, tokens, piece), f32),
        pltpu.VMEM((n // GROUP - 1, GROUP // 2, tokens, piece), f32),
        pltpu.VMEM((GROUP, tokens, piece), f32),
        pltpu.VMEM((GROUP, tokens, piece), f32),
        pltpu.VMEM((chips, tokens, piece), f32),
        pltpu.VMEM((chips, tokens, piece), f32),
        pltpu.VMEM((2, chips, own_rows + 16, head_dim), bf16),
        pltpu.VMEM((slots, share, own_rows, head_dim), bf16),
        pltpu.VMEM((128, 128), f32),
        pltpu.VMEM((n, own_rows, head_dim), bf16),
        pltpu.VMEM((n, own_rows, head_dim), bf16),
        pltpu.VMEM((n, 1, 128), f32),
        pltpu.VMEM((n, 1, 128), f32),
        pltpu.VMEM((n, 2 * tokens, width // 2), bf16),
        pltpu.VMEM((n, 2 * tokens, width // 2), bf16),
        pltpu.SemaphoreType.DMA((6,)),
        pltpu.SemaphoreType.DMA((3, n)),
        pltpu.SemaphoreType.DMA((2, 1 + requests)),
        pltpu.SemaphoreType.DMA((7 + requests, n)),
        pltpu.SemaphoreType.DMA((7 + requests, n)),
    ]
    return pl.pallas_call(
        step_kernel,
        out_shape=(
            pltpu.VMEM(hidden.shape, bf16),
            pltpu.VMEM((requests, drafts, kv_weight.shape[1]), bf16),
        ),
        in_specs=[hbm] * 13,
        out_specs=(vmem, vmem),
        scratch_shapes=scratch,
        compiler_params=pltpu.CompilerParams(
            collective_id=0, has_side_effects=True, vmem_limit_bytes=62 * 2**20
        ),
        name="decode_step",
    )(
        head_kind, cache_len, sink_len, window_len, hidden, norm_gain,
        q_weight, kv_weight, out_weight, ret_keys, ret_values, stream_keys, stream_values,
    )


def power_of_two(value):
    return value & (value - 1) == 0


def fused_fits(
    hidden, norm_gain, q_weight, kv_weight, out_weight, head_kind,
    ret_keys, ret_values, stream_keys, stream_values, cache_len, sink_len, window_len,
):
    n = lax.axis_size("seq")
    requests, drafts, width = hidden.shape
    tokens = requests * drafts
    head_dim = ret_keys.shape[3]
    own_width = out_weight.shape[0]
    kv_heads = head_kind.shape[0]
    heads = own_width // head_dim
    return (
        n % (2 * GROUP) == 0 and n <= 128 and n % kv_heads == 0 and tokens == 8
        and head_dim == 128 and width % 256 == 0 and own_width % head_dim == 0
        and q_weight.shape[1] == n * own_width and kv_weight.shape[1] == n * head_dim
        and n == 2 * kv_heads and power_of_two(heads * drafts) and power_of_two(drafts)
        and heads * drafts % 16 == 0 and 2 * tokens * heads <= 128
        and ret_keys.shape[2] % 128 == 0 and stream_keys.shape[2] % 128 == 0
        and ret_keys.shape[1] + stream_keys.shape[1] == kv_heads
    )


def step_device(*args):
    return fused_device(*args) if fused_fits(*args) else per_device(*args)


def solution(mesh):
    in_specs = (
        P("groups", None, "seq"),
        P("seq"),
        P("seq", None),
        P("seq", None),
        P("seq", None),
        P(),
        P("groups", None, "seq", None),
        P("groups", None, "seq", None),
        P("groups", None, "seq", None),
        P("groups", None, "seq", None),
        P("groups"),
        P("groups"),
        P("groups"),
    )
    out_specs = (P("groups", None, "seq"), P("groups", None, None))
    return jax.shard_map(
        step_device, mesh=mesh, in_specs=in_specs, out_specs=out_specs, check_vma=False
    )
```

```python
import math

import jax
import jax.numpy as jnp
from jax import lax
from jax.experimental import pallas as pl
from jax.experimental.pallas import tpu as pltpu
from jax.sharding import PartitionSpec as P

SINK_CAP = 128
MESH = pl.DeviceIdType.MESH
GROUP = 4


epsilon = 1e-05
floor_score = -1e30


def joined(part, axis, combine):
    gathered = jax.tree.map(lambda a: lax.all_gather(a, axis), part)

    def take(source):
        return jax.tree.map(lambda a: lax.dynamic_index_in_dim(a, source, 0, False), gathered)

    return lax.fori_loop(
        1, lax.axis_size(axis), lambda source, state: combine(state, take(source)), take(0)
    )


def block_stats(queries, cache_keys, cache_values, visible, score_scale):
    scores = (
        jnp.einsum("bhqd,bhld->bhql", queries, cache_keys, preferred_element_type=jnp.float32)
        * score_scale
    )
    scores = jnp.where(visible, scores, floor_score)
    peak_score = jnp.max(scores, axis=-1)
    weights = jnp.where(visible, jnp.exp(scores - peak_score[..., None]), 0.0)
    weight_total = jnp.sum(weights, axis=-1)
    block_out = jnp.einsum(
        "bhql,bhld->bhqd",
        weights.astype(jnp.bfloat16),
        cache_values,
        preferred_element_type=jnp.float32,
    )
    return (peak_score, weight_total, block_out)


def spread_rows(values_in, selector):
    return jnp.einsum("brq,gr->bgq", values_in, selector, precision=lax.Precision.HIGHEST)


def spread_vectors(values_in, selector):
    return jnp.einsum("brqd,gr->bgqd", values_in, selector, precision=lax.Precision.HIGHEST)


def join_parts(first_part, second_part):
    top_score = jnp.maximum(first_part[0], second_part[0])
    left_factor = jnp.exp(first_part[0] - top_score)
    right_factor = jnp.exp(second_part[0] - top_score)
    joined_total = first_part[1] * left_factor + second_part[1] * right_factor
    joined_out = first_part[2] * left_factor[..., None] + second_part[2] * right_factor[..., None]
    return (top_score, joined_total, joined_out)


def per_device(
    hidden,
    norm_gain,
    q_weight,
    kv_weight,
    out_weight,
    head_kind,
    ret_keys,
    ret_values,
    stream_keys,
    stream_values,
    cache_len,
    sink_len,
    window_len,
):
    requests, drafts, local_width = hidden.shape
    kv_heads = head_kind.shape[0]
    head_dim = ret_keys.shape[3]
    retrieval = ret_keys.shape[1]
    running = stream_keys.shape[1]
    head_count = q_weight.shape[1] // head_dim
    group_size = head_count // kv_heads
    query_rows = drafts * group_size
    devices = lax.axis_size("seq")
    position = lax.axis_index("seq")
    tokens = requests * drafts
    hidden32 = hidden.astype(jnp.float32)
    squares = lax.psum(jnp.sum(hidden32 * hidden32, axis=-1), "seq")
    inverse = lax.rsqrt(squares / (local_width * devices) + epsilon)
    normed = (hidden32 * inverse[..., None] * norm_gain.astype(jnp.float32)).astype(jnp.bfloat16)
    flat_rows = normed.reshape(tokens, local_width)
    part_query = jnp.dot(flat_rows, q_weight, preferred_element_type=jnp.float32)
    part_fresh = jnp.dot(flat_rows, kv_weight, preferred_element_type=jnp.float32)
    whole_query, whole_fresh = lax.psum((part_query, part_fresh), "seq")
    queries = whole_query.astype(jnp.bfloat16)
    new_entries = whole_fresh.astype(jnp.bfloat16)
    grouped = (
        queries.reshape(requests, drafts, kv_heads, group_size, head_dim)
        .transpose(0, 2, 1, 3, 4)
        .reshape(requests, kv_heads, query_rows, head_dim)
    )
    fresh_split = new_entries.reshape(requests, drafts, 2, kv_heads, head_dim)
    new_keys = fresh_split[:, :, 0].transpose(0, 2, 1, 3)
    new_values = fresh_split[:, :, 1].transpose(0, 2, 1, 3)
    kind_flag = head_kind == 1
    rank_ret = jnp.cumsum(head_kind) - 1
    rank_str = jnp.cumsum(1 - head_kind) - 1
    select_ret = (
        kind_flag[:, None] & (rank_ret[:, None] == jnp.arange(retrieval)[None, :])
    ).astype(jnp.float32)
    select_str = (
        jnp.logical_not(kind_flag)[:, None] & (rank_str[:, None] == jnp.arange(running)[None, :])
    ).astype(jnp.float32)
    ret_queries = jnp.einsum(
        "bgqd,gr->brqd",
        grouped,
        select_ret.astype(jnp.bfloat16),
        preferred_element_type=jnp.float32,
    ).astype(jnp.bfloat16)
    str_queries = jnp.einsum(
        "bgqd,gr->brqd",
        grouped,
        select_str.astype(jnp.bfloat16),
        preferred_element_type=jnp.float32,
    ).astype(jnp.bfloat16)
    score_scale = head_dim ** (-0.5)
    cache_block = ret_keys.shape[2]
    cache_pos = position * cache_block + jnp.arange(cache_block)
    ret_visible = (cache_pos[None, :] < cache_len[:, None])[:, None, None, :]
    slot_block = stream_keys.shape[2]
    slot_pos = (position * slot_block + jnp.arange(slot_block))[None, :]
    sink_part = slot_pos < sink_len[:, None]
    recent_part = (slot_pos >= SINK_CAP) & (slot_pos < SINK_CAP + window_len[:, None])
    str_visible = (sink_part | recent_part)[:, None, None, :]
    ret_peak, ret_total, ret_out = block_stats(
        ret_queries, ret_keys, ret_values, ret_visible, score_scale
    )
    str_peak, str_total, str_out = block_stats(
        str_queries, stream_keys, stream_values, str_visible, score_scale
    )
    peak_all = spread_rows(ret_peak, select_ret) + spread_rows(str_peak, select_str)
    total_all = spread_rows(ret_total, select_ret) + spread_rows(str_total, select_str)
    out_all = spread_vectors(ret_out, select_ret) + spread_vectors(str_out, select_str)
    token_of_row = jnp.arange(query_rows) // group_size
    new_visible = jnp.arange(drafts)[None, :] <= token_of_row[:, None]
    new_peak, new_total, new_out = block_stats(
        grouped, new_keys, new_values, new_visible, score_scale
    )
    own_width = out_weight.shape[0]
    cache_peak, cache_total, cache_out = joined((peak_all, total_all, out_all), "seq", join_parts)
    top_score = jnp.maximum(cache_peak, new_peak)
    cache_factor = jnp.exp(cache_peak - top_score)
    new_factor = jnp.exp(new_peak - top_score)
    denominator = cache_total * cache_factor + new_total * new_factor
    attended = (
        cache_out * cache_factor[..., None] + new_out * new_factor[..., None]
    ) / denominator[..., None]
    attention = (
        attended.reshape(requests, kv_heads, drafts, group_size, head_dim)
        .transpose(0, 2, 1, 3, 4)
        .reshape(tokens, head_count * head_dim)
        .astype(jnp.bfloat16)
    )
    own_attention = lax.dynamic_slice_in_dim(attention, position * own_width, own_width, 1)
    own_output = lax.psum_scatter(
        lax.dot_general(
            out_weight, own_attention, (((0,), (1,)), ((), ())), preferred_element_type=jnp.float32
        ),
        "seq",
        scatter_dimension=0,
        tiled=True,
    )
    layer_output = own_output.T.reshape(requests, drafts, local_width).astype(jnp.bfloat16)
    return (layer_output, new_entries.reshape(requests, drafts, 2 * kv_heads * head_dim))


def step_kernel(
    kind_hbm, clen_hbm, slen_hbm, wlen_hbm, hidden_hbm, gain_hbm,
    qw_hbm, kvw_hbm, ow_hbm, rk_hbm, rv_hbm, sk_hbm, sv_hbm,
    out_ref, new_ref,
    kind_ref, clen_ref, slen_ref, wlen_ref, hidden_ref, gain_ref,
    w_buf, o_buf, rk, rv, sk, sv,
    sq_send, sq_recv, sib_send, sib_recv, quad_send, quad_recv, rs_send, rs_recv, ag,
    a_res, stat_cols, a_send, a_recv, st_send, st_recv, o_send, o_recv,
    small_sem, load_sem, cache_sem, send_sem, recv_sem,
):
    f32, bf16 = jnp.float32, jnp.bfloat16
    n = lax.axis_size("seq")
    me = lax.axis_index("seq")
    core, chip, chips = lax.rem(me, 2), me // 2, n // 2
    sibling = me + 1 - 2 * core
    requests, drafts, width = hidden_ref.shape
    tokens = requests * drafts
    kv_heads = kind_ref.shape[0]
    retrieval, running = rk.shape[1], sk.shape[1]
    head_dim = rk.shape[3]
    own_width = o_buf.shape[1]
    piece = own_width + head_dim
    heads = own_width // head_dim
    share = n // kv_heads
    half_rows = heads * drafts
    own_rows = requests * half_rows
    group_rows = share * half_rows
    score_scale = head_dim ** (-0.5)
    exp_scale = score_scale * math.log2(math.e)
    SQ, SIB, RS, AG, STAT, OUT, QUAD, ATT = range(8)

    def remote(kind, src, dst, send_slot, recv_slot, target):
        return pltpu.make_async_remote_copy(
            src_ref=src, dst_ref=dst,
            send_sem=send_sem.at[kind, send_slot], recv_sem=recv_sem.at[kind, recv_slot],
            device_id={"seq": target}, device_id_type=MESH,
        )

    def peer(step):
        return lax.rem(me + step, n)

    def each_peer(body):
        for step in range(1, n):
            body(step, peer(step))

    def arrived(buffer, sem):
        span = buffer.at[pl.ds(1, n - 1)]
        pltpu.make_async_copy(span, span, sem).wait()

    slabs = n // GROUP
    own_slab = me // GROUP

    def slab(k):
        return lax.rem(own_slab + 1 + k, slabs)

    def columns(k, size):
        return pl.ds(pl.multiple_of(slab(k) * (GROUP * size), GROUP * size), GROUP * size)

    def weight_copies(k):
        return (
            pltpu.make_async_copy(
                qw_hbm.at[:, columns(k, own_width)],
                w_buf.at[k, :, pl.ds(0, GROUP * own_width)], load_sem.at[0, k]),
            pltpu.make_async_copy(
                kvw_hbm.at[:, columns(k, head_dim)],
                w_buf.at[k, :, pl.ds(GROUP * own_width, GROUP * head_dim)], load_sem.at[1, k]),
        )

    def out_copy(k):
        return pltpu.make_async_copy(
            ow_hbm.at[:, columns(k, width)], o_buf.at[k], load_sem.at[2, k])

    small = [
        pltpu.make_async_copy(src, dst, small_sem.at[at]) for at, (src, dst) in enumerate((
            (hidden_hbm, hidden_ref), (gain_hbm, gain_ref), (kind_hbm, kind_ref),
            (clen_hbm, clen_ref), (slen_hbm, slen_ref), (wlen_hbm, wlen_ref)))
    ]
    for copy in small:
        copy.start()
    barrier = pltpu.get_barrier_semaphore()
    each_peer(lambda step, target: pl.semaphore_signal(
        barrier, inc=1, device_id={"seq": target}, device_id_type=MESH))
    for k in range(slabs):
        for copy in weight_copies(k):
            copy.start()

    for copy in small:
        copy.wait()
    hidden32 = jnp.concatenate([hidden_ref[b].astype(f32) for b in range(requests)], axis=0)
    squares = jnp.sum(hidden32 * hidden32, axis=-1, keepdims=True)
    eye = (lax.broadcasted_iota(jnp.int32, (tokens, 128), 0)
           == lax.broadcasted_iota(jnp.int32, (tokens, 128), 1))
    sq_send[...] = jnp.sum(jnp.where(eye, squares, 0.0), axis=0, keepdims=True)
    sq_recv[0] = sq_send[...]
    stat_cols[...] = jnp.zeros_like(stat_cols)
    pl.semaphore_wait(barrier, n - 1)

    def sq_copy(step, target):
        return remote(SQ, sq_send, sq_recv.at[step], 0, 0, target)

    each_peer(lambda step, target: sq_copy(step, target).start())

    cache_copies = [
        (pltpu.make_async_copy(sk_hbm, sk, cache_sem.at[0, 0]),
         pltpu.make_async_copy(sv_hbm, sv, cache_sem.at[1, 0])),
    ]
    for b in range(requests):
        cache_copies.append(
            (pltpu.make_async_copy(rk_hbm.at[b], rk.at[b], cache_sem.at[0, 1 + b]),
             pltpu.make_async_copy(rv_hbm.at[b], rv.at[b], cache_sem.at[1, 1 + b])))
    for pair in cache_copies:
        for copy in pair:
            copy.start()
    arrived(sq_recv, recv_sem.at[SQ, 0])
    total_row = sq_recv[0]
    for s in range(1, n):
        total_row = total_row + sq_recv[s]
    total_sq = jnp.sum(jnp.where(eye, total_row, 0.0), axis=1, keepdims=True)
    inverse = lax.rsqrt(total_sq / (width * n) + epsilon)
    normed = (hidden32 * inverse * gain_ref[...].astype(f32).reshape(1, width)).astype(bf16)

    def part(whole, owner):
        return jnp.concatenate(
            [whole[:, owner * own_width:(owner + 1) * own_width],
             whole[:, GROUP * own_width + owner * head_dim:
                   GROUP * own_width + (owner + 1) * head_dim]], axis=1)

    def pick(flag, first, second):
        return jnp.where(flag == 0, first, second)

    def sib_copy(k):
        return remote(SIB, sib_send.at[k], sib_recv.at[k], k, k, sibling)

    pairs = GROUP // 2
    own_pair = lax.rem(chip, pairs)

    def rs_copy(k, u):
        target = 2 * (slab(k) * pairs + u) + core
        return remote(
            RS, rs_send.at[k * pairs + u], rs_recv.at[k * pairs + own_pair],
            k * pairs + u, k * pairs + own_pair, target)

    def rs_arrival(k, u):
        return remote(
            RS, rs_send.at[0], rs_recv.at[k * pairs + u], 0, k * pairs + u, sibling)

    own_at = lax.rem(me, GROUP)
    last = slabs - 1
    others = [lax.rem(own_at + hop, GROUP) for hop in range(1, GROUP)]

    def quad_copy(at):
        return remote(
            QUAD, quad_send.at[at], quad_recv.at[own_at], at, own_at, own_slab * GROUP + at)

    def quad_arrival(at):
        return remote(QUAD, quad_send.at[0], quad_recv.at[at], 0, at, sibling)

    mine = []

    def send_sums(k):
        sib_copy(k).wait_recv()
        for u in range(pairs):
            rs_send[k * pairs + u] = mine[k][u] + sib_recv[k, u]
            rs_copy(k, u).start()

    for k in range(slabs):
        for copy in weight_copies(k):
            copy.wait()
        whole = jnp.dot(normed, w_buf[k], preferred_element_type=f32)
        if k < last:
            sides = [(part(whole, 2 * u), part(whole, 2 * u + 1)) for u in range(pairs)]
            mine.append([pick(core, *side) for side in sides])
            for u in range(pairs):
                sib_send[k, u] = pick(core, sides[u][1], sides[u][0])
            sib_copy(k).start()
        else:
            for at in range(GROUP):
                quad_send[at] = part(whole, at)
            for at in others:
                quad_copy(at).start()
        if k > 0:
            send_sums(k - 1)

    own = quad_send[own_at]

    for k in range(slabs):
        out_copy(k).start()

    for k in range(last):
        for u in range(pairs):
            rs_arrival(k, u).wait_recv()
            own = own + rs_recv[k * pairs + u]
    for at in others:
        quad_arrival(at).wait_recv()
        own = own + quad_recv[at]

    def by_head(values):
        return jnp.concatenate(
            [values[b * drafts:(b + 1) * drafts, h * head_dim:(h + 1) * head_dim]
             for b in range(requests) for h in range(heads)], axis=0)

    packed = jnp.concatenate(
        [by_head(own[:, :own_width]), own[:, own_width:],
         jnp.zeros((ag.shape[2] - own_rows - tokens, head_dim), f32)], axis=0)
    ag[core, chip] = packed.astype(bf16)

    def ag_copy(step, target, source):
        return remote(
            AG, ag.at[core, source], ag.at[core, source], step, source, 2 * target + core)

    def each_chip(body):
        for step in range(1, chips):
            body(step, lax.rem(chip + step, chips))

    def pair_copy(side):
        return remote(AG, ag.at[side], ag.at[side], chips, chips, sibling)

    each_chip(lambda step, target: ag_copy(step, target, chip).start())

    kinds = [kind_ref[g] for g in range(kv_heads)]
    slot_of, before = [], 0
    for g in range(kv_heads):
        slot = jnp.where(kinds[g] == 1, before, retrieval + g - before)
        slot_of.append(jnp.minimum(slot, retrieval + running - 1))
        before = before + kinds[g]
    head_of = []
    for j in range(retrieval + running):
        found = 0
        for g in range(kv_heads):
            found = found + jnp.where(slot_of[g] == j, g, 0)
        head_of.append(jnp.minimum(found, kv_heads - 1))

    each_chip(lambda step, source: ag_copy(step, source, source).wait_recv())
    pair_copy(core).start()
    pair_copy(1 - core).wait_recv()

    for p in range(n):
        entries = ag[p % 2, p // 2, own_rows:, :]
        for b in range(requests):
            new_ref[b, :, p * head_dim:(p + 1) * head_dim] = entries[b * drafts:(b + 1) * drafts]

    def score(b, j, keys):
        q = jnp.concatenate(
            [ag[s % 2, head_of[j] * share // 2 + s // 2, b * half_rows:(b + 1) * half_rows, :]
             for s in range(share)], axis=0)
        return lax.dot_general(q, keys, (((1,), (1,)), ((), ())), preferred_element_type=f32)

    def attend(parts):
        scores = [jnp.where(seen, score(b, j, keys), floor_score)
                  for b, j, keys, _, seen in parts]
        peaks = [jnp.max(found, axis=-1, keepdims=True) for found in scores]
        weights = [jnp.exp2((found - peak) * exp_scale) for found, peak in zip(scores, peaks)]
        totals = [jnp.sum(weight, axis=-1, keepdims=True) for weight in weights]
        blocks = [jnp.dot(weight.astype(bf16), part[3], preferred_element_type=f32)
                  for weight, part in zip(weights, parts)]
        for part, block in zip(parts, blocks):
            b, j = part[0], part[1]
            a_res[j, :, b * half_rows:(b + 1) * half_rows, :] = block.astype(bf16).reshape(
                share, half_rows, head_dim)
        lane = lax.broadcasted_iota(jnp.int32, (half_rows, 128), 1)
        for b in sorted({part[0] for part in parts}):
            for at, columns_of in ((0, peaks), (own_rows, totals)):
                rows = pl.ds(at + b * half_rows, half_rows)
                kept = stat_cols[rows, :]
                for part, column in zip(parts, columns_of):
                    if part[0] == b:
                        for s in range(share):
                            kept = jnp.where(lane == share * head_of[part[1]] + s,
                                             column[s * half_rows:(s + 1) * half_rows], kept)
                stat_cols[rows, :] = kept

    for copy in cache_copies[0]:
        copy.wait()
    slots = sk.shape[2]
    slot_pos = me * slots + lax.broadcasted_iota(jnp.int32, (1, slots), 1)
    positions = rk.shape[2]
    cache_pos = me * positions + lax.broadcasted_iota(jnp.int32, (1, positions), 1)
    small_parts = []
    for b in range(requests):
        seen = (slot_pos < slen_ref[b]) | (
            (slot_pos >= SINK_CAP) & (slot_pos < SINK_CAP + wlen_ref[b]))
        for r in range(running):
            small_parts.append((b, retrieval + r, sk[b, r], sv[b, r], seen))
    attend(small_parts)

    def att_copy(b, step, target):
        rows = pl.ds(b * half_rows, half_rows)
        return remote(ATT + b, a_send.at[target, rows], a_recv.at[step, rows], 0, 0, target)

    for b in range(requests):
        for copy in cache_copies[1 + b]:
            copy.wait()
        seen = cache_pos < clen_ref[b]
        attend([(b, r, rk[b, r], rv[b, r], seen) for r in range(retrieval)])
        rows = slice(b * half_rows, (b + 1) * half_rows)
        for g in range(kv_heads):
            a_send[g * share:(g + 1) * share, rows] = a_res[slot_of[g], :, rows]
        a_recv[0, rows] = a_send[me, rows]
        if b < requests - 1:
            each_peer(lambda step, target: att_copy(b, step, target).start())

    lane = lax.broadcasted_iota(jnp.int32, (128, 128), 0)
    stat_rows = jnp.where(lane < own_rows, stat_cols[...] * score_scale, stat_cols[...]).T
    for p in range(n):
        st_send[p] = stat_rows[p:p + 1, :]
    st_recv[0] = st_send[me]

    def st_copy(step, target):
        return remote(STAT, st_send.at[target], st_recv.at[step], 0, 0, target)

    each_peer(lambda step, target: st_copy(step, target).start())
    each_peer(lambda step, target: att_copy(requests - 1, step, target).start())

    own_head = me // share
    own_q = ag[core, chip, 0:own_rows, :]
    new_keys = ag[lax.rem(own_head, 2), own_head // 2, own_rows:, :]
    new_values = ag[lax.rem(kv_heads + own_head, 2), (kv_heads + own_head) // 2, own_rows:, :]
    new_rows = ag.shape[2] - own_rows
    scores = lax.dot_general(own_q, new_keys, (((1,), (1,)), ((), ())), preferred_element_type=f32)
    scores = scores * score_scale
    row = lax.broadcasted_iota(jnp.int32, (own_rows, new_rows), 0)
    col = lax.broadcasted_iota(jnp.int32, (own_rows, new_rows), 1)
    row_bits, col_bits = half_rows.bit_length() - 1, drafts.bit_length() - 1
    same = lax.shift_right_logical(row, row_bits) == lax.shift_right_logical(col, col_bits)
    visible = same & ((col & (drafts - 1)) <= (row & (drafts - 1)))
    scores = jnp.where(visible, scores, floor_score)
    new_peak = jnp.max(scores, axis=-1, keepdims=True)
    new_weights = jnp.where(visible, jnp.exp(scores - new_peak), 0.0)
    new_total = jnp.sum(new_weights, axis=-1, keepdims=True)
    new_out = jnp.dot(new_weights.astype(bf16), new_values, preferred_element_type=f32)

    arrived(st_recv, recv_sem.at[STAT, 0])
    stats = jnp.concatenate(
        [st_recv[s] for s in range(n)] + [jnp.zeros((128 - n, 128), f32)], axis=0).T
    lane = lax.broadcasted_iota(jnp.int32, (own_rows, 128), 1)
    peaks = jnp.where(lane < n, stats[0:own_rows], floor_score)
    totals = stats[own_rows:2 * own_rows]
    top = jnp.maximum(jnp.max(peaks, axis=-1, keepdims=True), new_peak)
    factors = jnp.exp(peaks - top)
    new_factor = jnp.exp(new_peak - top)
    denominator = jnp.sum(factors * totals, axis=-1, keepdims=True) + new_factor * new_total
    numerator = new_factor * new_out
    for b in range(requests):
        arrived(a_recv.at[:, pl.ds(b * half_rows, half_rows)], recv_sem.at[ATT + b, 0])
    for s in range(n):
        numerator = numerator + factors[:, s:s + 1] * a_recv[s].astype(f32)
    attended = numerator / denominator
    attention = jnp.concatenate(
        [jnp.concatenate(
            [attended[b * half_rows + h * drafts:b * half_rows + (h + 1) * drafts]
             for b in range(requests)], axis=0) for h in range(heads)], axis=1).astype(bf16)

    half_width = width // 2

    def o_copy(k, at):
        owner = slab(k) * GROUP + at
        slot = k * GROUP + lax.rem(me, GROUP)
        return remote(OUT, o_send.at[k * GROUP + at], o_recv.at[slot], k * GROUP + at, slot, owner)

    def o_arrival(k, at):
        slot = k * GROUP + at
        return remote(OUT, o_send.at[0], o_recv.at[slot], 0, slot, sibling)

    for k in range(slabs):
        out_copy(k).wait()
        whole = jnp.dot(attention, o_buf[k], preferred_element_type=f32)
        for at in range(GROUP):
            begin = at * width
            o_send[k * GROUP + at] = jnp.concatenate(
                [whole[:, begin:begin + half_width], whole[:, begin + half_width:begin + width]],
                axis=0).astype(bf16)
            if k < slabs - 1:
                o_copy(k, at).start()
    for hop in range(1, GROUP):
        o_copy(slabs - 1, lax.rem(own_at + hop, GROUP)).start()
    result = o_send[(slabs - 1) * GROUP + own_at].astype(f32)
    for k in range(slabs):
        for at in range(GROUP):
            if k < slabs - 1:
                o_arrival(k, at).wait_recv()
                result = result + o_recv[k * GROUP + at].astype(f32)
            elif at > 0:
                place = lax.rem(own_at + at, GROUP)
                o_arrival(k, place).wait_recv()
                result = result + o_recv[k * GROUP + place].astype(f32)
    result = jnp.concatenate([result[:tokens], result[tokens:]], axis=1).astype(bf16)
    for b in range(requests):
        out_ref[b] = result[b * drafts:(b + 1) * drafts]

    arrived(sq_recv, send_sem.at[SQ, 0])
    arrived(st_recv, send_sem.at[STAT, 0])
    for b in range(requests):
        arrived(a_recv.at[:, pl.ds(b * half_rows, half_rows)], send_sem.at[ATT + b, 0])
    each_chip(lambda step, target: ag_copy(step, target, chip).wait_send())
    pair_copy(core).wait_send()
    for k in range(last):
        sib_copy(k).wait_send()
        for u in range(pairs):
            rs_copy(k, u).wait_send()
        for at in range(GROUP):
            o_copy(k, at).wait_send()
    for at in others:
        quad_copy(at).wait_send()
    for hop in range(1, GROUP):
        o_copy(last, lax.rem(own_at + hop, GROUP)).wait_send()


def fused_device(
    hidden, norm_gain, q_weight, kv_weight, out_weight, head_kind,
    ret_keys, ret_values, stream_keys, stream_values, cache_len, sink_len, window_len,
):
    n = lax.axis_size("seq")
    requests, drafts, width = hidden.shape
    tokens = requests * drafts
    head_dim = ret_keys.shape[3]
    own_width = out_weight.shape[0]
    own_rows = tokens * (own_width // head_dim)
    slots = ret_keys.shape[1] + stream_keys.shape[1]
    share = n // slots
    chips = n // 2
    piece = own_width + head_dim
    f32, bf16 = jnp.float32, jnp.bfloat16
    vmem = pl.BlockSpec(memory_space=pltpu.VMEM)
    hbm = pl.BlockSpec(memory_space=pltpu.HBM)
    scratch = [
        pltpu.SMEM(head_kind.shape, jnp.int32),
        pltpu.SMEM(cache_len.shape, jnp.int32),
        pltpu.SMEM(sink_len.shape, jnp.int32),
        pltpu.SMEM(window_len.shape, jnp.int32),
        pltpu.VMEM(hidden.shape, bf16),
        pltpu.VMEM(norm_gain.shape, bf16),
        pltpu.VMEM((n // GROUP, width, GROUP * piece), bf16),
        pltpu.VMEM((n // GROUP, own_width, GROUP * width), bf16),
        pltpu.VMEM(ret_keys.shape, bf16),
        pltpu.VMEM(ret_values.shape, bf16),
        pltpu.VMEM(stream_keys.shape, bf16),
        pltpu.VMEM(stream_values.shape, bf16),
        pltpu.VMEM((1, 128), f32),
        pltpu.VMEM((n, 1, 128), f32),
        pltpu.VMEM((n // GROUP - 1, GROUP // 2, tokens, piece), f32),
        pltpu.VMEM((n // GROUP - 1, GROUP // 2, tokens, piece), f32),
        pltpu.VMEM((GROUP, tokens, piece), f32),
        pltpu.VMEM((GROUP, tokens, piece), f32),
        pltpu.VMEM((chips, tokens, piece), f32),
        pltpu.VMEM((chips, tokens, piece), f32),
        pltpu.VMEM((2, chips, own_rows + 16, head_dim), bf16),
        pltpu.VMEM((slots, share, own_rows, head_dim), bf16),
        pltpu.VMEM((128, 128), f32),
        pltpu.VMEM((n, own_rows, head_dim), bf16),
        pltpu.VMEM((n, own_rows, head_dim), bf16),
        pltpu.VMEM((n, 1, 128), f32),
        pltpu.VMEM((n, 1, 128), f32),
        pltpu.VMEM((n, 2 * tokens, width // 2), bf16),
        pltpu.VMEM((n, 2 * tokens, width // 2), bf16),
        pltpu.SemaphoreType.DMA((6,)),
        pltpu.SemaphoreType.DMA((3, n)),
        pltpu.SemaphoreType.DMA((2, 1 + requests)),
        pltpu.SemaphoreType.DMA((7 + requests, n)),
        pltpu.SemaphoreType.DMA((7 + requests, n)),
    ]
    return pl.pallas_call(
        step_kernel,
        out_shape=(
            pltpu.VMEM(hidden.shape, bf16),
            pltpu.VMEM((requests, drafts, kv_weight.shape[1]), bf16),
        ),
        in_specs=[hbm] * 13,
        out_specs=(vmem, vmem),
        scratch_shapes=scratch,
        compiler_params=pltpu.CompilerParams(
            collective_id=0, has_side_effects=True, vmem_limit_bytes=62 * 2**20
        ),
        name="decode_step",
    )(
        head_kind, cache_len, sink_len, window_len, hidden, norm_gain,
        q_weight, kv_weight, out_weight, ret_keys, ret_values, stream_keys, stream_values,
    )


def power_of_two(value):
    return value & (value - 1) == 0


def fused_fits(
    hidden, norm_gain, q_weight, kv_weight, out_weight, head_kind,
    ret_keys, ret_values, stream_keys, stream_values, cache_len, sink_len, window_len,
):
    n = lax.axis_size("seq")
    requests, drafts, width = hidden.shape
    tokens = requests * drafts
    head_dim = ret_keys.shape[3]
    own_width = out_weight.shape[0]
    kv_heads = head_kind.shape[0]
    heads = own_width // head_dim
    return (
        n % (2 * GROUP) == 0 and n <= 128 and n % kv_heads == 0 and tokens == 8
        and head_dim == 128 and width % 256 == 0 and own_width % head_dim == 0
        and q_weight.shape[1] == n * own_width and kv_weight.shape[1] == n * head_dim
        and n == 2 * kv_heads and power_of_two(heads * drafts) and power_of_two(drafts)
        and heads * drafts % 16 == 0 and 2 * tokens * heads <= 128
        and ret_keys.shape[2] % 128 == 0 and stream_keys.shape[2] % 128 == 0
        and ret_keys.shape[1] + stream_keys.shape[1] == kv_heads
    )


def step_device(*args):
    return fused_device(*args) if fused_fits(*args) else per_device(*args)


def solution(mesh):
    in_specs = (
        P("groups", None, "seq"),
        P("seq"),
        P("seq", None),
        P("seq", None),
        P("seq", None),
        P(),
        P("groups", None, "seq", None),
        P("groups", None, "seq", None),
        P("groups", None, "seq", None),
        P("groups", None, "seq", None),
        P("groups"),
        P("groups"),
        P("groups"),
    )
    out_specs = (P("groups", None, "seq"), P("groups", None, None))
    return jax.shard_map(
        step_device, mesh=mesh, in_specs=in_specs, out_specs=out_specs, check_vma=False
    )
```
